32 devices in a mesh: groups: 2 (over y), seq: 16 (over z, x, core).
Axes of the slice: x: 2, y: 2, z: 4, core: 2. Of those that a mesh axis runs over, the one named last changes fastest.
Arguments:
- token_ids: int32 [4096], P('groups'), parts along dimension 0, may hold values from 0 to 511
- vocab_table: bfloat16 [512, 3, 4096], P(None, None, 'seq'), may hold values from -6 to 6
- short_filter: float32 [7, 3, 4096], replicated, may hold values from -2 to 2
- residue: float32 [4096, 16], replicated, may hold values from -1.5 to 1.5
- decay: float32 [4096, 16], replicated, may hold values from 0.2 to 64
- skip_gain: float32 [4096], replicated, may hold values from -3 to 3
Outputs:
- hyena_out: bfloat16 [4096, 4096], P(('groups', 'seq')), parts along dimension 0
The draws below stay inside these ranges and needn't reach their ends.
There are 2 independent parts, one for each index of `groups`. The reference program is written for one: setup_inputs(seed, part) draws one part's arguments, and reference() takes and returns one part's arrays. A program takes and returns all parts, laid end to end along the dimension named above; an argument that names none is the same for every part. Nothing has to cross between parts.
All inputs are finite; a program needn't handle non-finite values.
Results may differ from the reference program's by a relative error of at most 0.012.
Values may be sent and summed in bfloat16 or wider, within the bound.
No kernel may reach another device: no remote copies, remote signals or barrier semaphores. Data moves between devices by JAX's collectives and lax.ppermute only.
A program may use at most 192 MiB of HBM per device.

```python
import math
import jax
import jax.numpy as jnp
from jax import lax

D = 4096
VOCAB = 512
SHORT = 7
POLES = 16
SEQ_LEN = 2048


def plant(entries, stream_key, least, top_value):
    spot = [jax.random.randint(jax.random.fold_in(stream_key, axis), (), 0, length) for axis, length in enumerate(entries.shape)]
    main_axis = entries.shape.index(max(entries.shape))
    neighbour = spot[:main_axis] + [(spot[main_axis] + 1) % entries.shape[main_axis]] + spot[main_axis + 1:]
    return entries.at[tuple(spot)].set(least).at[tuple(neighbour)].set(top_value)


def shard_levels(own_key, extent, split, least, high):
    loudness, own = 1.0, jax.random.fold_in(own_key, 6)
    for dim, blocks in split:
        steps = jnp.exp(jax.random.uniform(jax.random.fold_in(own, dim), (blocks,), jnp.float32, least / len(split), high / len(split)))
        loudness = loudness * jnp.repeat(steps, extent[dim] // blocks).reshape([-1 if axis == dim else 1 for axis in range(len(extent))])
    return loudness


def gaussian(stream_key, dims, scale, limit, cuts=(), kind=jnp.bfloat16):
    array = jax.random.normal(stream_key, dims, jnp.float32) * scale
    if len(cuts) > 0:
        array = shard_levels(stream_key, dims, cuts, -0.22, 0.18) * array
    return jnp.clip(array, min=-limit, max=limit).astype(kind)


def setup_inputs(seed: int = 0, part: int = 0) -> dict:
    splits = jax.random.split(jax.random.key(seed), 7)
    part_keys = jax.random.split(jax.random.fold_in(splits[6], part), 7)
    token_ids = plant(jax.random.randint(part_keys[0], (SEQ_LEN,), 0, VOCAB), jax.random.fold_in(part_keys[0], 1), 0, VOCAB - 1).astype(jnp.int32)
    vocab_table = gaussian(splits[1], (VOCAB, 3, D), 1.0, 6.0, ((2, 16),))
    short_filter = gaussian(splits[2], (SHORT, 3, D), SHORT ** -0.5, 2.0, (), jnp.float32)
    residue = gaussian(splits[3], (D, POLES), 0.25, 1.5, (), jnp.float32)
    decay = jnp.clip(jnp.exp(jax.random.uniform(splits[4], (D, POLES), jnp.float32, math.log(0.2), math.log(64.0))), 0.2, 64.0)
    skip_gain = gaussian(splits[5], (D,), 0.5, 3.0, (), jnp.float32)
    return {"token_ids": token_ids, "vocab_table": vocab_table, "short_filter": short_filter, "residue": residue, "decay": decay, "skip_gain": skip_gain}


def filter_spectrum(freq, total, pole, gap, tail, scale):
    theta = freq.astype(jnp.float32) * (2.0 * math.pi / total)
    sine = jnp.sin(theta)[:, None]
    halfsq = (jnp.sin(0.5 * theta) ** 2)[:, None]
    parity = (1 - 2 * (freq % 2)).astype(jnp.float32)[:, None]
    real_part = jnp.zeros((freq.shape[0], pole.shape[0]), jnp.float32)
    imag_part = jnp.zeros((freq.shape[0], pole.shape[0]), jnp.float32)
    for mode in range(pole.shape[1]):
        dreal = gap[:, mode] + 2.0 * pole[:, mode] * halfsq
        dimag = pole[:, mode] * sine
        factor = scale[:, mode] * (1.0 - tail[:, mode] * parity) / (dreal * dreal + dimag * dimag)
        real_part = real_part + factor * dreal
        imag_part = imag_part - factor * dimag
    return (real_part, imag_part)

def reference(token_ids, vocab_table, short_filter, residue, decay, skip_gain):
    length = token_ids.shape[0]
    total = 2 * length
    streams = jnp.take(vocab_table, token_ids, axis=0).astype(jnp.float32)
    rim = short_filter.shape[0] - 1
    padded = jnp.pad(streams, ((rim, 0), (0, 0), (0, 0)))
    mixed = jnp.zeros(streams.shape, jnp.float32)
    for lag in range(rim + 1):
        mixed = mixed + short_filter[lag] * padded[rim - lag:rim - lag + length]
    query = mixed[:, 0]
    gated = mixed[:, 1] * mixed[:, 2]
    rate = decay / length
    pole = jnp.exp(-rate)
    gap = -jnp.expm1(-rate)
    tail = jnp.exp(-decay)
    scale = residue * jnp.sqrt(2.0 * rate)
    width = gated.shape[1]
    group = min(width, 256)
    count = width // group
    modes = pole.shape[1]

    def one_block(items):
        block_gated, block_pole, block_gap, block_tail, block_scale = items
        spectrum_gated = jnp.fft.rfft(block_gated, n=total, axis=0)
        freq = jnp.arange(length + 1, dtype=jnp.int32)
        filt_real, filt_imag = filter_spectrum(freq, total, block_pole, block_gap, block_tail, block_scale)
        product = spectrum_gated * lax.complex(filt_real, filt_imag)
        return jnp.fft.irfft(product, n=total, axis=0)[:length]
    blocks = gated.reshape(length, count, group).transpose(1, 0, 2)
    convolved = lax.map(one_block, (blocks, pole.reshape(count, group, modes), gap.reshape(count, group, modes), tail.reshape(count, group, modes), scale.reshape(count, group, modes)))
    convolved = convolved.transpose(1, 0, 2).reshape(length, width)
    result = convolved + skip_gain * gated
    return (query * result).astype(jnp.bfloat16)
```

```python
import functools

import jax
import jax.numpy as jnp
from jax import lax
from jax.experimental import pallas as pl
from jax.experimental.pallas import tpu as pltpu
from jax.sharding import PartitionSpec as P

LANES = 128
RUNS = 8


def tree_sum(terms):
    while len(terms) > 1:
        pairs = [a + b for a, b in zip(terms[::2], terms[1::2])]
        terms = pairs + ([terms[-1]] if len(terms) % 2 else [])
    return terms[0]


def delay_runs(value, by):
    moved = pltpu.roll(value, by, 0)
    return jnp.where(lax.broadcasted_iota(jnp.int32, value.shape, 0) < by, 0.0, moved)


def operator(ids, table, taps, residue, decay, skip, out, onehot, streams, query, gated, result):
    steps = ids.shape[1]
    vocab = table.shape[1]
    width = taps.shape[0]
    modes = residue.shape[0]
    rim = width - 1
    length = steps * RUNS
    tile = (RUNS, LANES)

    cols = min(LANES, steps)
    part = min(32, cols)
    word = lax.broadcasted_iota(jnp.int32, (RUNS, vocab), 1)

    def look_up(block, _):
        here = ids[:, pl.ds(pl.multiple_of(block * cols, cols), cols)]
        for first in range(0, cols, part):
            hot = [
                jnp.where(jnp.broadcast_to(here[:, j : j + 1], word.shape) == word, 1.0, 0.0)
                for j in range(first, first + part)
            ]
            onehot[...] = jnp.concatenate(hot, axis=0).astype(jnp.bfloat16)
            row = (rim + block * cols + first) * RUNS
            row = pl.multiple_of(row, RUNS)
            for k in range(3):
                streams[k, pl.ds(row, part * RUNS), :] = jnp.dot(
                    onehot[...], table[k], preferred_element_type=jnp.float32
                )
        return 0

    lax.fori_loop(0, steps // cols, look_up, 0)
    for k in range(3):
        for j in range(rim):
            streams[k, j * RUNS : (j + 1) * RUNS, :] = delay_runs(
                streams[k, (steps + j) * RUNS : (steps + j + 1) * RUNS, :], 1
            )

    def mix(j, _):
        mixed = []
        for k in range(3):
            terms = []
            for lag in range(width):
                row = pl.multiple_of((j + rim - lag) * RUNS, RUNS)
                tap = jnp.broadcast_to(taps[lag, k : k + 1, :], tile)
                terms.append(tap * streams[k, pl.ds(row, RUNS), :])
            mixed.append(tree_sum(terms))
        row = pl.multiple_of(j * RUNS, RUNS)
        query[pl.ds(row, RUNS), :] = mixed[0]
        gated[pl.ds(row, RUNS), :] = mixed[1] * mixed[2]
        return 0

    lax.fori_loop(0, steps, mix, 0, unroll=8)

    rate = decay[...] / length
    weight = residue[...] * jnp.sqrt(2.0 * rate)
    pole = jnp.exp(-rate)
    spread = lambda rows, s: jnp.broadcast_to(rows[s : s + 1, :], tile)
    poles = [spread(pole, s) for s in range(modes)]
    weights = [spread(weight, s) for s in range(modes)]

    def advance(j, state):
        now = gated[pl.ds(pl.multiple_of(j * RUNS, RUNS), RUNS), :]
        return tuple(p * x + now for p, x in zip(poles, state))

    zero = jnp.zeros(tile, jnp.float32)
    ends = lax.fori_loop(0, steps, advance, (zero,) * modes, unroll=8)
    begins = []
    for s in range(modes):
        value = delay_runs(ends[s], 1)
        by = 1
        while by < RUNS:
            leap = spread(jnp.exp(-rate * (steps * by)), s)
            value = value + leap * delay_runs(value, by)
            by *= 2
        begins.append(value)
    direct = jnp.broadcast_to(skip[...], tile)

    def emit(j, state):
        row = pl.multiple_of(j * RUNS, RUNS)
        now = gated[pl.ds(row, RUNS), :]
        state = tuple(p * x + now for p, x in zip(poles, state))
        total = tree_sum([w * x for w, x in zip(weights, state)])
        result[pl.ds(j, RUNS, stride=steps), :] = query[pl.ds(row, RUNS), :] * (total + direct * now)
        return state

    lax.fori_loop(0, steps, emit, tuple(begins), unroll=8)
    out[...] = result[...].astype(jnp.bfloat16)


def run_operator(ids, table, taps, residue, decay, skip, piece):
    steps = ids.shape[1]
    length = steps * RUNS
    rim = taps.shape[0] - 1
    part = min(32, steps)
    chan = lambda *lead: pl.BlockSpec(lead + (LANES,), lambda i: (0,) * len(lead) + (piece,))
    return pl.pallas_call(
        operator,
        grid=(1,),
        out_shape=jax.ShapeDtypeStruct((length, LANES), jnp.bfloat16),
        in_specs=[
            pl.BlockSpec(ids.shape, lambda i: (0, 0)),
            chan(*table.shape[:2]),
            chan(*taps.shape[:2]),
            chan(residue.shape[0]),
            chan(decay.shape[0]),
            chan(1),
        ],
        out_specs=pl.BlockSpec((length, LANES), lambda i: (0, 0)),
        scratch_shapes=[
            pltpu.VMEM((part * RUNS, table.shape[1]), jnp.bfloat16),
            pltpu.VMEM((3, length + rim * RUNS, LANES), jnp.float32),
            pltpu.VMEM((length, LANES), jnp.float32),
            pltpu.VMEM((length, LANES), jnp.float32),
            pltpu.VMEM((length, LANES), jnp.float32),
        ],
        compiler_params=pltpu.CompilerParams(vmem_limit_bytes=56 * 2**20),
        cost_estimate=pl.CostEstimate(flops=length * LANES * 8000, bytes_accessed=4 * 2**20, transcendentals=0),
    )(ids, table, taps, residue, decay, skip)


def body(token_ids, vocab_table, short_filter, residue, decay, skip_gain):
    places = lax.axis_size("seq")
    place = lax.axis_index("seq")
    length = token_ids.shape[0]
    local = length // places
    share = vocab_table.shape[2]
    pieces = -(-share // LANES)
    widen = lambda x: jnp.pad(x, [(0, 0)] * (x.ndim - 1) + [(0, pieces * LANES - share)])
    mine = lambda x, axis: lax.dynamic_slice_in_dim(x, place * share, share, axis)
    ids = token_ids.reshape(RUNS, length // RUNS)
    table = widen(vocab_table.transpose(1, 0, 2))
    taps = widen(mine(short_filter, 2))
    res = widen(mine(residue, 0).T)
    dec = widen(mine(decay, 0).T)
    skip = widen(mine(skip_gain, 0)[None])
    parts = []
    for piece in range(pieces):
        outcome = run_operator(ids, table, taps, res, dec, skip, piece)
        kept = min(LANES, share - piece * LANES)
        sent = outcome[:, :kept].reshape(places, local, kept)
        parts.append(lax.all_to_all(sent, "seq", split_axis=0, concat_axis=0, tiled=True))
    joined = jnp.concatenate(parts, axis=2)
    return joined.transpose(1, 0, 2).reshape(local, places * share)


def solution(mesh):
    placed = (P("groups"), P(None, None, "seq"), P(), P(), P(), P())
    return jax.shard_map(
        body, mesh=mesh, in_specs=placed, out_specs=P(("groups", "seq"), None), check_vma=False
    )
```

```python
import math

import jax
import jax.numpy as jnp
from jax import lax
from jax.experimental import pallas as pl
from jax.experimental.pallas import tpu as pltpu
from jax.sharding import PartitionSpec as P

LANES = 128
RUNS = 8


def tree_sum(terms):
    while len(terms) > 1:
        pairs = [a + b for a, b in zip(terms[::2], terms[1::2])]
        terms = pairs + ([terms[-1]] if len(terms) % 2 else [])
    return terms[0]


def delay_runs(value, by):
    moved = pltpu.roll(value, by, 0)
    return jnp.where(lax.broadcasted_iota(jnp.int32, value.shape, 0) < by, 0.0, moved)


def operator(spot, ids, table, taps, residue, decay, skip, *rest):
    outs, (onehot, streams, query, gated, result) = rest[:-5], rest[-5:]
    length = ids.shape[0] * ids.shape[1]
    steps = length // RUNS
    vocab = table.shape[1]
    width = taps.shape[1]
    modes = residue.shape[0]
    rim = width - 1
    tile = (RUNS, LANES)

    cols = ids.shape[1]
    part = onehot.shape[0] // RUNS
    word = lax.broadcasted_iota(jnp.int32, (RUNS, vocab), 1)

    def look_up(block, _):
        here = ids[pl.ds(block, RUNS, stride=steps // cols), :]
        for first in range(0, cols, part):
            hot = [
                jnp.where(jnp.broadcast_to(here[:, j : j + 1], word.shape) == word, 1.0, 0.0)
                for j in range(first, first + part)
            ]
            onehot[...] = jnp.concatenate(hot, axis=0).astype(jnp.bfloat16)
            row = (rim + block * cols + first) * RUNS
            row = pl.multiple_of(row, RUNS)
            for k in range(3):
                streams[k, pl.ds(row, part * RUNS), :] = jnp.dot(
                    onehot[...], table[k], preferred_element_type=jnp.float32
                )
        return 0

    lax.fori_loop(0, steps // cols, look_up, 0)
    for k in range(3):
        for j in range(rim):
            streams[k, j * RUNS : (j + 1) * RUNS, :] = delay_runs(
                streams[k, (steps + j) * RUNS : (steps + j + 1) * RUNS, :], 1
            )

    def mix(j, _):
        mixed = []
        for k in range(3):
            terms = []
            for lag in range(width):
                row = pl.multiple_of((j + rim - lag) * RUNS, RUNS)
                tap = jnp.broadcast_to(taps[k, lag : lag + 1, :], tile)
                terms.append(tap * streams[k, pl.ds(row, RUNS), :])
            mixed.append(tree_sum(terms))
        row = pl.multiple_of(j * RUNS, RUNS)
        query[pl.ds(row, RUNS), :] = mixed[0]
        gated[pl.ds(row, RUNS), :] = mixed[1] * mixed[2]
        return 0

    lax.fori_loop(0, steps, mix, 0, unroll=8)

    rate = decay[...] / length
    weight = residue[...] * jnp.sqrt(2.0 * rate)
    pole = jnp.exp(-rate)
    spread = lambda rows, s: jnp.broadcast_to(rows[s : s + 1, :], tile)
    poles = [spread(pole, s) for s in range(modes)]
    weights = [spread(weight, s) for s in range(modes)]

    def advance(j, state):
        now = gated[pl.ds(pl.multiple_of(j * RUNS, RUNS), RUNS), :]
        return tuple(p * x + now for p, x in zip(poles, state))

    zero = jnp.zeros(tile, jnp.float32)
    ends = lax.fori_loop(0, steps, advance, (zero,) * modes, unroll=8)
    begins = []
    for s in range(modes):
        value = delay_runs(ends[s], 1)
        by = 1
        while by < RUNS:
            leap = spread(jnp.exp(-rate * (steps * by)), s)
            value = value + leap * delay_runs(value, by)
            by *= 2
        begins.append(value)
    direct = jnp.broadcast_to(skip[...], tile)

    def emit(j, state):
        row = pl.multiple_of(j * RUNS, RUNS)
        now = gated[pl.ds(row, RUNS), :]
        state = tuple(p * x + now for p, x in zip(poles, state))
        total = tree_sum([w * x for w, x in zip(weights, state)])
        result[pl.ds(j, RUNS, stride=steps), :] = query[pl.ds(row, RUNS), :] * (total + direct * now)
        return state

    lax.fori_loop(0, steps, emit, tuple(begins), unroll=8)
    size = length // len(outs)
    for d, out in enumerate(outs):
        first = pl.multiple_of(jnp.bitwise_xor(spot[1], d) * size, size) if len(outs) > 1 else 0
        out[...] = result[pl.ds(first, size), :].astype(jnp.bfloat16)


def run_operator(spot, ids, table, taps, residue, decay, skip, piece, pieces, blocks):
    length = ids.size
    rim = taps.shape[1] - 1
    part = min(32, ids.shape[1])
    own = lambda *lead: pl.BlockSpec(lead + (LANES,), lambda i, spot: (0,) * len(lead) + (piece,))
    all_own = lambda *lead: pl.BlockSpec(
        lead + (LANES,), lambda i, spot: (0,) * len(lead) + (spot[0] * pieces + piece,)
    )
    size = length // blocks
    return pl.pallas_call(
        operator,
        grid_spec=pltpu.PrefetchScalarGridSpec(
            num_scalar_prefetch=1,
            grid=(1,),
            in_specs=[
                pl.BlockSpec(ids.shape, lambda i, spot: (0, 0)),
                own(*table.shape[:2]),
                all_own(*taps.shape[:2]),
                all_own(residue.shape[0]),
                all_own(decay.shape[0]),
                all_own(1),
            ],
            out_specs=[pl.BlockSpec((size, LANES), lambda i, spot: (0, 0))] * blocks,
            scratch_shapes=[
                pltpu.VMEM((part * RUNS, table.shape[1]), jnp.bfloat16),
                pltpu.VMEM((3, length + rim * RUNS, LANES), jnp.float32),
                pltpu.VMEM((length, LANES), jnp.float32),
                pltpu.VMEM((length, LANES), jnp.float32),
                pltpu.VMEM((length, LANES), jnp.float32),
            ],
        ),
        out_shape=[jax.ShapeDtypeStruct((size, LANES), jnp.bfloat16)] * blocks,
        compiler_params=pltpu.CompilerParams(vmem_limit_bytes=56 * 2**20),
        cost_estimate=pl.CostEstimate(flops=length * LANES * 8000, bytes_accessed=4 * 2**20, transcendentals=0),
    )(spot, ids, table, taps, residue, decay, skip)


def join(spot, *refs):
    out = refs[-1]
    last = refs[-2]
    hops = refs[:-2]
    places, _, kept = last.shape
    far = hops[0].shape[0]
    near = places // far
    group = (len(hops) // near + 1) * kept
    for source in range(places):
        first = source * group + group - kept
        out[:, first : first + kept] = last[source]
    for k, hop in enumerate(hops):
        piece, e = k // near, k % near
        for d in range(far):
            source = jnp.bitwise_xor(spot[1], d) * near + jnp.bitwise_xor(spot[2], e)
            first = pl.multiple_of(source * group + piece * kept, kept)
            out[:, pl.ds(first, kept)] = hop[d]


def spread_far(blocks, far, near, local):
    kept = blocks[0].shape[1]
    count = far * near
    spread = [blocks[0]] + [
        lax.ppermute(blocks[d], "seq", [(i, i ^ (near * d)) for i in range(count)]) for d in range(1, far)
    ]
    return [x.reshape(near, local, kept) for x in spread]


def spread_near(spread, near, place, count):
    hops = []
    for e in range(near):
        chosen = jnp.stack([lax.dynamic_index_in_dim(x, (place % near) ^ e, 0, False) for x in spread])
        hops.append(lax.ppermute(chosen, "seq", [(i, i ^ e) for i in range(count)]) if e else chosen)
    return hops


def body(token_ids, vocab_table, short_filter, residue, decay, skip_gain):
    places = lax.axis_size("seq")
    place = lax.axis_index("seq")
    length = token_ids.shape[0]
    local = length // places
    share = vocab_table.shape[2]
    pieces = -(-share // LANES)
    near = math.gcd(places, 4)
    far = places // near
    ids = token_ids.reshape(-1, min(LANES, length // RUNS))
    table = vocab_table.transpose(1, 0, 2)
    rows = [short_filter.transpose(1, 0, 2), residue.T, decay.T, skip_gain[None]]
    column = place
    if share % LANES:
        widen = lambda x: jnp.pad(x, [(0, 0)] * (x.ndim - 1) + [(0, pieces * LANES - share)])
        rows = [widen(lax.dynamic_slice_in_dim(x, place * share, share, x.ndim - 1)) for x in rows]
        table = widen(table)
        column = 0 * place
    spot = jnp.stack([column, place // near, place % near]).astype(jnp.int32)
    staged = share % LANES == 0 and far & (far - 1) == 0 and pieces > 1
    waiting = []
    hops = []
    parts = []
    for piece in range(pieces):
        by_hops = staged and piece < pieces - 1
        blocks = run_operator(spot, ids, table, *rows, piece, pieces, far if by_hops else 1)
        if by_hops:
            *blocks, spot = lax.optimization_barrier((*blocks, spot))
            waiting.append(spread_far(blocks, far, near, local))
            continue
        kept = min(LANES, share - piece * LANES)
        sent = blocks[0][:, :kept].reshape(places, local, kept)
        if staged:
            sent, waiting = lax.optimization_barrier((sent, waiting))
        parts.append(lax.all_to_all(sent, "seq", split_axis=0, concat_axis=0, tiled=True))
    if not staged:
        return jnp.concatenate(parts, axis=2).transpose(1, 0, 2).reshape(local, places * share)
    for spread in waiting:
        hops += spread_near(spread, near, place, places)
    whole = pl.BlockSpec(memory_space=pltpu.VMEM)
    return pl.pallas_call(
        join,
        in_specs=[pl.BlockSpec(memory_space=pltpu.SMEM)] + [whole] * (len(hops) + 1),
        out_specs=whole,
        out_shape=jax.ShapeDtypeStruct((local, places * share), jnp.bfloat16),
        compiler_params=pltpu.CompilerParams(vmem_limit_bytes=16 * 2**20),
    )(spot, *hops, *parts)


def solution(mesh):
    placed = (P("groups"), P(None, None, "seq"), P(), P(), P(), P())
    return jax.shard_map(
        body, mesh=mesh, in_specs=placed, out_specs=P(("groups", "seq"), None), check_vma=False
    )
```

```python
import functools
import math

import jax
import jax.numpy as jnp
from jax import lax
from jax.experimental import pallas as pl
from jax.experimental.pallas import tpu as pltpu
from jax.sharding import PartitionSpec as P

LANES = 128
RUNS = 8


def tree_sum(terms):
    while len(terms) > 1:
        pairs = [a + b for a, b in zip(terms[::2], terms[1::2])]
        terms = pairs + ([terms[-1]] if len(terms) % 2 else [])
    return terms[0]


def delay_runs(value, by):
    moved = pltpu.roll(value, by, 0)
    return jnp.where(lax.broadcasted_iota(jnp.int32, value.shape, 0) < by, 0.0, moved)


def operator(spot, *refs):
    piece, pieces, near, sliced, blocks, raw, ahead = spot
    place = lax.axis_index("seq")
    refs = list(refs)
    take = lambda count: [refs.pop(0) for _ in range(count)]
    given, outs = take(6), take(blocks)
    ahead = take(6) if ahead else []
    if raw:
        held, sem = take(6), take(1)[0]

        def bring(first, into, which):
            column = first * LANES if sliced else (place * pieces + first) * LANES
            own = pl.ds(pl.multiple_of(column, LANES), LANES)
            ids, table, taps, residue, decay, skip = given
            pairs = [(ids, into[0])]
            for k in range(3):
                pairs.append((table.at[k, :, pl.ds(first * LANES, LANES)], into[1].at[:, pl.ds(k * LANES, LANES)]))
            pairs.append((taps.at[:, :, own], into[2]))
            for ref, target in zip((residue, decay, skip), into[3:]):
                pairs.append((ref.at[:, own], target))
            return [pltpu.make_async_copy(x, y, sem.at[which, n]) for n, (x, y) in enumerate(pairs)]

        now = bring(piece, held, 0)
        later = bring(piece + 1, ahead, 1) if ahead else []
        for copy in now + later:
            copy.start()
        for copy in now:
            copy.wait()
    else:
        held, later = given, []
    compute(place // near, held, outs, *refs)
    for copy in later:
        copy.wait()


def compute(far_place, held, outs, halo, query, gated, inputs, factors, result, *streams):
    ids, table, taps, residue, decay, skip = held
    length = ids.shape[0] * ids.shape[1]
    steps = length // RUNS
    vocab = table.shape[0]
    width = taps.shape[1]
    modes = residue.shape[0]
    rim = width - 1
    tile = (RUNS, LANES)
    spread = lambda row: jnp.broadcast_to(row, tile)

    cols = ids.shape[1]
    part = cols // len(streams)
    word = lax.broadcasted_iota(jnp.int32, (RUNS, vocab), 1)

    def look_up(here, first, count):
        hot = [
            jnp.where(jnp.broadcast_to(here[:, j : j + 1], word.shape) == word, 1.0, 0.0)
            for j in range(first, first + count)
        ]
        hot = jnp.concatenate(hot, axis=0).astype(jnp.bfloat16)
        found = jnp.dot(hot, table[...], preferred_element_type=jnp.float32)
        return [found[:, k * LANES : (k + 1) * LANES] for k in range(3)]

    def ids_of(block):
        return ids[pl.ds(block, RUNS, stride=steps // cols), :]

    tail = look_up(ids_of(steps // cols - 1), cols - rim, rim)
    for k in range(3):
        for j in range(rim):
            rows = slice(j * RUNS, (j + 1) * RUNS)
            halo[k, rows, :] = delay_runs(tail[k][rows], 1)

    filters = [[spread(taps[k, lag : lag + 1, :]) for lag in range(width)] for k in range(3)]

    def block_step(block, _):
        here = ids_of(block)
        seen = {}

        def row(k, j):
            if (k, j) not in seen:
                if j < 0:
                    seen[k, j] = halo[k, (rim + j) * RUNS : (rim + j + 1) * RUNS, :]
                else:
                    first = j % part * RUNS
                    seen[k, j] = streams[j // part][k, first : first + RUNS, :]
            return seen[k, j]

        def mix(first):
            for j in range(first, first + part):
                mixed = [
                    tree_sum([filters[k][lag] * row(k, j - lag) for lag in range(width)]) for k in range(3)
                ]
                at = pl.ds(pl.multiple_of((block * cols + j) * RUNS, RUNS), RUNS)
                query[at, :] = mixed[0]
                gated[at, :] = mixed[1] * mixed[2]

        for n, stream in enumerate(streams):
            for k, found in enumerate(look_up(here, n * part, part)):
                stream[k] = found
            if n > 0:
                mix((n - 1) * part)
        mix(cols - part)
        for k in range(3):
            halo[k] = streams[-1][k, (part - rim) * RUNS :, :]
        return 0

    lax.fori_loop(0, steps // cols, block_step, 0)

    batch = factors.shape[0] // modes
    rate = decay[...] / length
    weight = residue[...] * jnp.sqrt(2.0 * rate)
    pole = jnp.exp(-rate)
    power = weight
    early = []
    for n in range(batch):
        early.append(spread(jnp.sum(power, axis=0, keepdims=True)))
        power = weight * jnp.exp(-rate * (n + 1))
        for s in range(modes):
            factors[n * modes + s] = spread(power[s : s + 1])
    early[0] = early[0] + spread(skip[...])
    poles = [spread(pole[s : s + 1]) for s in range(modes)]
    leap = jnp.exp(-rate * batch)
    leaps = [spread(leap[s : s + 1]) for s in range(modes)]

    def tokens(ref, m):
        first = m * batch
        return [ref[pl.ds(pl.multiple_of((first + n) * RUNS, RUNS), RUNS), :] for n in range(batch)]

    def advance(m, state):
        values = tokens(gated, m)
        after = []
        for s in range(modes):
            taken = values[0]
            for value in values[1:]:
                taken = poles[s] * taken + value
            inputs[s, pl.ds(pl.multiple_of(m * RUNS, RUNS), RUNS), :] = taken
            after.append(leaps[s] * state[s] + taken)
        return tuple(after)

    zero = jnp.zeros(tile, jnp.float32)
    ends = lax.fori_loop(0, steps // batch, advance, (zero,) * modes, unroll=4)
    begins = []
    for s in range(modes):
        value = delay_runs(ends[s], 1)
        by = 1
        while by < RUNS:
            value = value + spread(jnp.exp(-rate[s : s + 1] * (steps * by))) * delay_runs(value, by)
            by *= 2
        begins.append(value)

    def emit(m, state):
        values = tokens(gated, m)
        for n, asked in enumerate(tokens(query, m)):
            terms = [early[lag] * values[n - lag] for lag in range(n + 1)]
            terms += [factors[n * modes + s] * state[s] for s in range(modes)]
            result[pl.ds(m * batch + n, RUNS, stride=steps), :] = asked * tree_sum(terms)
        at = pl.ds(pl.multiple_of(m * RUNS, RUNS), RUNS)
        return tuple(leaps[s] * state[s] + inputs[s, at, :] for s in range(modes))

    lax.fori_loop(0, steps // batch, emit, tuple(begins), unroll=4)
    size = length // len(outs)
    for d, out in enumerate(outs):
        first = pl.multiple_of(jnp.bitwise_xor(far_place, d) * size, size) if len(outs) > 1 else 0
        out[...] = result[pl.ds(first, size), :].astype(jnp.bfloat16)


def run_operator(given, piece, pieces, near, sliced, blocks):
    ids, table, taps, residue = given[:4]
    raw = piece == 0 or pieces > 2
    ahead = piece == 0 and pieces == 2
    vocab, modes, width = table.shape[-2], residue.shape[0], taps.shape[1]
    length = ids.size
    steps = length // RUNS
    cols = ids.shape[1]
    parts = max(cols // 32, 1)
    batch = max(4, steps // 128)
    inside = pl.BlockSpec(memory_space=pltpu.VMEM)
    outside = pl.BlockSpec(memory_space=pl.ANY)
    floats = lambda *shape: pltpu.VMEM(shape + (LANES,), jnp.float32)
    own = [
        jax.ShapeDtypeStruct(ids.shape, jnp.int32),
        jax.ShapeDtypeStruct((vocab, 3 * LANES), jnp.bfloat16),
        jax.ShapeDtypeStruct((3, width, LANES), jnp.float32),
        jax.ShapeDtypeStruct((modes, LANES), jnp.float32),
        jax.ShapeDtypeStruct((modes, LANES), jnp.float32),
        jax.ShapeDtypeStruct((1, LANES), jnp.float32),
    ]
    out_shape = [jax.ShapeDtypeStruct((length // blocks, LANES), jnp.bfloat16)] * blocks
    scratch = []
    if raw:
        scratch = [pltpu.VMEM(x.shape, x.dtype) for x in own] + [pltpu.SemaphoreType.DMA((2, 8))]
        out_shape = out_shape + (own if ahead else [])
    results = pl.pallas_call(
        functools.partial(operator, (piece, pieces, near, sliced, blocks, raw, ahead)),
        in_specs=[outside if raw else inside] * 6,
        out_specs=[inside] * len(out_shape),
        out_shape=out_shape,
        scratch_shapes=scratch
        + [
            floats(3, (width - 1) * RUNS),
            floats(length),
            floats(length),
            floats(modes, steps // batch * RUNS),
            floats(batch * modes, RUNS),
            floats(length),
        ]
        + [floats(3, cols // parts * RUNS)] * parts,
        compiler_params=pltpu.CompilerParams(vmem_limit_bytes=56 * 2**20),
        cost_estimate=pl.CostEstimate(flops=length * LANES * 8000, bytes_accessed=4 * 2**20, transcendentals=0),
    )(*given)
    return results[:blocks], results[blocks:]


def join(piece, pieces, *refs):
    refs, out, sem = refs[:-2], refs[-2], refs[-1]
    place = lax.axis_index("seq")
    copies = []
    kept = refs[0].shape[-1]
    for e, ref in enumerate(refs):
        for d in range(ref.shape[0]):
            source = d if piece == pieces - 1 else jnp.bitwise_xor(place, d * len(refs) + e)
            first = pl.multiple_of((source * pieces + piece) * kept, kept)
            copies.append(pltpu.make_async_copy(ref.at[d], out.at[:, pl.ds(first, kept)], sem.at[len(copies)]))
    for copy in copies:
        copy.start()
    for copy in copies:
        copy.wait()


def run_join(piece, pieces, blocks, out):
    count = sum(x.shape[0] for x in blocks)
    inside = pl.BlockSpec(memory_space=pltpu.VMEM)
    outside = pl.BlockSpec(memory_space=pl.ANY)
    into = [] if out is None else [out]

    def kernel(*refs):
        refs = list(refs)
        if into:
            refs.pop(len(blocks))
        join(piece, pieces, *refs)

    local, kept = blocks[0].shape[1:]
    return pl.pallas_call(
        kernel,
        in_specs=[inside] * len(blocks) + [outside] * len(into),
        out_specs=outside,
        out_shape=jax.ShapeDtypeStruct((local, count * pieces * kept), blocks[0].dtype),
        scratch_shapes=[pltpu.SemaphoreType.DMA((count,))],
        input_output_aliases={len(blocks): 0} if into else {},
        compiler_params=pltpu.CompilerParams(vmem_limit_bytes=2**20),
    )(*blocks, *into)


def spread_far(blocks, far, near, local):
    kept = blocks[0].shape[1]
    count = far * near
    spread = [blocks[0]] + [
        lax.ppermute(blocks[d], "seq", [(i, i ^ (near * d)) for i in range(count)]) for d in range(1, far)
    ]
    return [x.reshape(near, local, kept) for x in spread]


def spread_near(spread, near, place, count):
    hops = []
    for e in range(near):
        chosen = jnp.stack([lax.dynamic_index_in_dim(x, (place % near) ^ e, 0, False) for x in spread])
        hops.append(lax.ppermute(chosen, "seq", [(i, i ^ e) for i in range(count)]) if e else chosen)
    return hops


def body(token_ids, vocab_table, short_filter, residue, decay, skip_gain):
    places = lax.axis_size("seq")
    place = lax.axis_index("seq")
    length = token_ids.shape[0]
    local = length // places
    share = vocab_table.shape[2]
    pieces = -(-share // LANES)
    near = math.gcd(places, 4)
    far = places // near
    ids = token_ids.reshape(-1, min(LANES, length // RUNS))
    table = vocab_table.transpose(1, 0, 2)
    rows = [short_filter.transpose(1, 0, 2), residue.T, decay.T, skip_gain[None]]
    sliced = share % LANES != 0
    if sliced:
        widen = lambda x: jnp.pad(x, [(0, 0)] * (x.ndim - 1) + [(0, pieces * LANES - share)])
        rows = [widen(lax.dynamic_slice_in_dim(x, place * share, share, x.ndim - 1)) for x in rows]
        table = widen(table)
    staged = not sliced and far & (far - 1) == 0 and pieces > 1
    given = (ids, table, *rows)
    waiting = []
    parts = []
    for piece in range(pieces):
        by_hops = staged and piece < pieces - 1
        blocks, ahead = run_operator(given, piece, pieces, near, sliced, far if by_hops else 1)
        given = ahead or given
        if by_hops:
            waiting.append(spread_far(blocks, far, near, local))
            continue
        kept = min(LANES, share - piece * LANES)
        sent = blocks[0][:, :kept].reshape(places, local, kept)
        if staged:
            sent, waiting = lax.optimization_barrier((sent, waiting))
        parts.append(lax.all_to_all(sent, "seq", split_axis=0, concat_axis=0, tiled=True))
    if not staged:
        return jnp.concatenate(parts, axis=2).transpose(1, 0, 2).reshape(local, places * share)
    out = None
    for piece, spread in enumerate(waiting):
        out = run_join(piece, pieces, spread_near(spread, near, place, places), out)
    return run_join(pieces - 1, pieces, parts, out)


def solution(mesh):
    placed = (P("groups"), P(None, None, "seq"), P(), P(), P(), P())
    return jax.shard_map(
        body, mesh=mesh, in_specs=placed, out_specs=P(("groups", "seq"), None), check_vma=False
    )
```

```python
import functools
import math

import jax
import jax.numpy as jnp
from jax import lax
from jax.experimental import pallas as pl
from jax.experimental.pallas import tpu as pltpu
from jax.sharding import PartitionSpec as P

LANES = 128
RUNS = 8


def tree_sum(terms):
    while len(terms) > 1:
        pairs = [a + b for a, b in zip(terms[::2], terms[1::2])]
        terms = pairs + ([terms[-1]] if len(terms) % 2 else [])
    return terms[0]


def delay_runs(value, by):
    moved = pltpu.roll(value, by, 0)
    return jnp.where(lax.broadcasted_iota(jnp.int32, value.shape, 0) < by, 0.0, moved)


def operator(spot, *refs):
    piece, pieces, near, sliced, blocks, raw, ahead = spot
    place = lax.axis_index("seq")
    refs = list(refs)
    take = lambda count: [refs.pop(0) for _ in range(count)]
    given, outs = take(6), take(blocks)
    ahead = take(6) if ahead else []
    if raw:
        held, sem = take(6), take(1)[0]

        def bring(first, into, which):
            column = first * LANES if sliced else (place * pieces + first) * LANES
            own = pl.ds(pl.multiple_of(column, LANES), LANES)
            ids, table, taps, residue, decay, skip = given
            pairs = [(ids, into[0])]
            for k in range(3):
                pairs.append((table.at[k, :, pl.ds(first * LANES, LANES)], into[1].at[:, pl.ds(k * LANES, LANES)]))
            pairs.append((taps.at[:, :, own], into[2]))
            for ref, target in zip((residue, decay, skip), into[3:]):
                pairs.append((ref.at[:, own], target))
            return [pltpu.make_async_copy(x, y, sem.at[which, n]) for n, (x, y) in enumerate(pairs)]

        now = bring(piece, held, 0)
        later = bring(piece + 1, ahead, 1) if ahead else []
        for copy in now + later:
            copy.start()
        for copy in now:
            copy.wait()
    else:
        held, later = given, []
    compute(place // near, held, outs, *refs)
    for copy in later:
        copy.wait()


def compute(far_place, held, outs, halo, query, gated, inputs, factors, result, *streams):
    ids, table, taps, residue, decay, skip = held
    length = ids.shape[0] * ids.shape[1]
    steps = length // RUNS
    vocab = table.shape[0]
    width = taps.shape[1]
    modes = residue.shape[0]
    rim = width - 1
    tile = (RUNS, LANES)
    spread = lambda row: jnp.broadcast_to(row, tile)

    cols = ids.shape[1]
    part = cols // len(streams)
    word = lax.broadcasted_iota(jnp.int32, (RUNS, vocab), 1)

    def look_up(here, first, count):
        hot = [
            jnp.where(jnp.broadcast_to(here[:, j : j + 1], word.shape) == word, 1.0, 0.0)
            for j in range(first, first + count)
        ]
        hot = jnp.concatenate(hot, axis=0).astype(jnp.bfloat16)
        found = jnp.dot(hot, table[...], preferred_element_type=jnp.float32)
        return [found[:, k * LANES : (k + 1) * LANES] for k in range(3)]

    def ids_of(block):
        return ids[pl.ds(block, RUNS, stride=steps // cols), :]

    tail = look_up(ids_of(steps // cols - 1), cols - rim, rim)
    for k in range(3):
        for j in range(rim):
            rows = slice(j * RUNS, (j + 1) * RUNS)
            halo[k, rows, :] = delay_runs(tail[k][rows], 1)

    filters = [[spread(taps[k, lag : lag + 1, :]) for lag in range(width)] for k in range(3)]

    def block_step(block, _):
        here = ids_of(block)
        seen = {}

        def row(k, j):
            if (k, j) not in seen:
                if j < 0:
                    seen[k, j] = halo[k, (rim + j) * RUNS : (rim + j + 1) * RUNS, :]
                else:
                    first = j % part * RUNS
                    seen[k, j] = streams[j // part][k, first : first + RUNS, :]
            return seen[k, j]

        def mix(first):
            for j in range(first, first + part):
                mixed = [
                    tree_sum([filters[k][lag] * row(k, j - lag) for lag in range(width)]) for k in range(3)
                ]
                at = pl.ds(pl.multiple_of((block * cols + j) * RUNS, RUNS), RUNS)
                query[at, :] = mixed[0]
                gated[at, :] = mixed[1] * mixed[2]

        for n, stream in enumerate(streams):
            for k, found in enumerate(look_up(here, n * part, part)):
                stream[k] = found
            if n > 0:
                mix((n - 1) * part)
        mix(cols - part)
        for k in range(3):
            halo[k] = streams[-1][k, (part - rim) * RUNS :, :]
        return 0

    lax.fori_loop(0, steps // cols, block_step, 0)

    batch = factors.shape[0] // modes
    rate = decay[...] / length
    weight = residue[...] * jnp.sqrt(2.0 * rate)
    pole = jnp.exp(-rate)
    power = weight
    early = []
    for n in range(batch):
        early.append(spread(jnp.sum(power, axis=0, keepdims=True)))
        power = weight * jnp.exp(-rate * (n + 1))
        for s in range(modes):
            factors[n * modes + s] = spread(power[s : s + 1])
    early[0] = early[0] + spread(skip[...])
    poles = [spread(pole[s : s + 1]) for s in range(modes)]
    leap = jnp.exp(-rate * batch)
    leaps = [spread(leap[s : s + 1]) for s in range(modes)]

    def tokens(ref, m):
        first = m * batch
        return [ref[pl.ds(pl.multiple_of((first + n) * RUNS, RUNS), RUNS), :] for n in range(batch)]

    def advance(m, state):
        values = tokens(gated, m)
        after = []
        for s in range(modes):
            taken = values[0]
            for value in values[1:]:
                taken = poles[s] * taken + value
            inputs[s, pl.ds(pl.multiple_of(m * RUNS, RUNS), RUNS), :] = taken
            after.append(leaps[s] * state[s] + taken)
        return tuple(after)

    zero = jnp.zeros(tile, jnp.float32)
    ends = lax.fori_loop(0, steps // batch, advance, (zero,) * modes, unroll=4)
    begins = []
    for s in range(modes):
        value = delay_runs(ends[s], 1)
        by = 1
        while by < RUNS:
            value = value + spread(jnp.exp(-rate[s : s + 1] * (steps * by))) * delay_runs(value, by)
            by *= 2
        begins.append(value)

    def emit(m, state):
        values = tokens(gated, m)
        for n, asked in enumerate(tokens(query, m)):
            terms = [early[lag] * values[n - lag] for lag in range(n + 1)]
            terms += [factors[n * modes + s] * state[s] for s in range(modes)]
            result[pl.ds(m * batch + n, RUNS, stride=steps), :] = asked * tree_sum(terms)
        at = pl.ds(pl.multiple_of(m * RUNS, RUNS), RUNS)
        return tuple(leaps[s] * state[s] + inputs[s, at, :] for s in range(modes))

    lax.fori_loop(0, steps // batch, emit, tuple(begins), unroll=4)
    size = length // len(outs)
    for d, out in enumerate(outs):
        first = pl.multiple_of(jnp.bitwise_xor(far_place, d) * size, size) if len(outs) > 1 else 0
        out[...] = result[pl.ds(first, size), :].astype(jnp.bfloat16)


def run_operator(given, piece, pieces, near, sliced, blocks):
    ids, table, taps, residue = given[:4]
    raw = piece == 0 or pieces > 2
    ahead = piece == 0 and pieces == 2
    vocab, modes, width = table.shape[-2], residue.shape[0], taps.shape[1]
    length = ids.size
    steps = length // RUNS
    cols = ids.shape[1]
    parts = max(cols // 32, 1)
    batch = max(4, steps // 128)
    inside = pl.BlockSpec(memory_space=pltpu.VMEM)
    outside = pl.BlockSpec(memory_space=pltpu.HBM)
    floats = lambda *shape: pltpu.VMEM(shape + (LANES,), jnp.float32)
    own = [
        jax.ShapeDtypeStruct(ids.shape, jnp.int32),
        jax.ShapeDtypeStruct((vocab, 3 * LANES), jnp.bfloat16),
        jax.ShapeDtypeStruct((3, width, LANES), jnp.float32),
        jax.ShapeDtypeStruct((modes, LANES), jnp.float32),
        jax.ShapeDtypeStruct((modes, LANES), jnp.float32),
        jax.ShapeDtypeStruct((1, LANES), jnp.float32),
    ]
    out_shape = [jax.ShapeDtypeStruct((length // blocks, LANES), jnp.bfloat16)] * blocks
    scratch = []
    if raw:
        scratch = [pltpu.VMEM(x.shape, x.dtype) for x in own] + [pltpu.SemaphoreType.DMA((2, 8))]
        out_shape = out_shape + (own if ahead else [])
    scratch += [
        floats(3, (width - 1) * RUNS),
        floats(length),
        floats(length),
        floats(modes, steps // batch * RUNS),
        floats(batch * modes, RUNS),
        floats(length),
    ]
    scratch += [floats(3, cols // parts * RUNS)] * parts
    held = scratch + own * 2 + out_shape
    room = sum(math.prod(x.shape) * jnp.dtype(x.dtype).itemsize for x in held if x.dtype in (jnp.float32, jnp.bfloat16))
    results = pl.pallas_call(
        functools.partial(operator, (piece, pieces, near, sliced, blocks, raw, ahead)),
        in_specs=[outside if raw else inside] * 6,
        out_specs=[inside] * len(out_shape),
        out_shape=out_shape,
        scratch_shapes=scratch,
        compiler_params=pltpu.CompilerParams(vmem_limit_bytes=room + 4 * 2**20),
        cost_estimate=pl.CostEstimate(flops=length * LANES * 8000, bytes_accessed=4 * 2**20, transcendentals=0),
    )(*(given if not raw else [pltpu.with_memory_space_constraint(x, pltpu.HBM) for x in given]))
    return results[:blocks], results[blocks:]


def join(piece, pieces, *refs):
    refs, out, sem = refs[:-2], refs[-2], refs[-1]
    place = lax.axis_index("seq")
    copies = []
    kept = refs[0].shape[-1]
    for e, ref in enumerate(refs):
        for d in range(ref.shape[0]):
            source = d if piece == pieces - 1 else jnp.bitwise_xor(place, d * len(refs) + e)
            first = pl.multiple_of((source * pieces + piece) * kept, kept)
            copies.append(pltpu.make_async_copy(ref.at[d], out.at[:, pl.ds(first, kept)], sem.at[len(copies)]))
    for copy in copies:
        copy.start()
    for copy in copies:
        copy.wait()


def run_join(piece, pieces, blocks, out):
    count = sum(x.shape[0] for x in blocks)
    inside = pl.BlockSpec(memory_space=pltpu.VMEM)
    outside = pl.BlockSpec(memory_space=pl.ANY)
    into = [] if out is None else [out]

    def kernel(*refs):
        refs = list(refs)
        if into:
            refs.pop(len(blocks))
        join(piece, pieces, *refs)

    local, kept = blocks[0].shape[1:]
    return pl.pallas_call(
        kernel,
        in_specs=[inside] * len(blocks) + [outside] * len(into),
        out_specs=outside,
        out_shape=jax.ShapeDtypeStruct((local, count * pieces * kept), blocks[0].dtype),
        scratch_shapes=[pltpu.SemaphoreType.DMA((count,))],
        input_output_aliases={len(blocks): 0} if into else {},
        compiler_params=pltpu.CompilerParams(vmem_limit_bytes=2**20),
    )(*blocks, *into)


def spread_far(blocks, far, near, local):
    kept = blocks[0].shape[1]
    count = far * near
    spread = [blocks[0]] + [
        lax.ppermute(blocks[d], "seq", [(i, i ^ (near * d)) for i in range(count)]) for d in range(1, far)
    ]
    return [x.reshape(near, local, kept) for x in spread]


def spread_near(spread, near, place, count):
    hops = []
    for e in range(near):
        chosen = jnp.stack([lax.dynamic_index_in_dim(x, (place % near) ^ e, 0, False) for x in spread])
        hops.append(lax.ppermute(chosen, "seq", [(i, i ^ e) for i in range(count)]) if e else chosen)
    return hops


def body(token_ids, vocab_table, short_filter, residue, decay, skip_gain):
    places = lax.axis_size("seq")
    place = lax.axis_index("seq")
    length = token_ids.shape[0]
    local = length // places
    share = vocab_table.shape[2]
    pieces = -(-share // LANES)
    near = math.gcd(places, 4)
    far = places // near
    ids = token_ids.reshape(-1, min(LANES, length // RUNS))
    table = vocab_table.transpose(1, 0, 2)
    rows = [short_filter.transpose(1, 0, 2), residue.T, decay.T, skip_gain[None]]
    sliced = share % LANES != 0
    if sliced:
        widen = lambda x: jnp.pad(x, [(0, 0)] * (x.ndim - 1) + [(0, pieces * LANES - share)])
        rows = [widen(lax.dynamic_slice_in_dim(x, place * share, share, x.ndim - 1)) for x in rows]
        table = widen(table)
    staged = not sliced and far & (far - 1) == 0 and pieces > 1
    given = (ids, table, *rows)
    waiting = []
    parts = []
    for piece in range(pieces):
        by_hops = staged and piece < pieces - 1
        blocks, ahead = run_operator(given, piece, pieces, near, sliced, far if by_hops else 1)
        given = ahead or given
        if by_hops:
            waiting.append(spread_far(blocks, far, near, local))
            continue
        kept = min(LANES, share - piece * LANES)
        sent = blocks[0][:, :kept].reshape(places, local, kept)
        if staged:
            sent, waiting = lax.optimization_barrier((sent, waiting))
        parts.append(lax.all_to_all(sent, "seq", split_axis=0, concat_axis=0, tiled=True))
    if not staged:
        return jnp.concatenate(parts, axis=2).transpose(1, 0, 2).reshape(local, places * share)
    out = None
    for piece, spread in enumerate(waiting):
        out = run_join(piece, pieces, spread_near(spread, near, place, places), out)
    return run_join(pieces - 1, pieces, parts, out)


def solution(mesh):
    placed = (P("groups"), P(None, None, "seq"), P(), P(), P(), P())
    return jax.shard_map(
        body, mesh=mesh, in_specs=placed, out_specs=P(("groups", "seq"), None), check_vma=False
    )
```

```python
import functools
import math

import jax
import jax.numpy as jnp
from jax import lax
from jax.experimental import pallas as pl
from jax.experimental.pallas import tpu as pltpu
from jax.sharding import PartitionSpec as P

LANES = 128
RUNS = 8


def tree_sum(terms):
    while len(terms) > 1:
        pairs = [a + b for a, b in zip(terms[::2], terms[1::2])]
        terms = pairs + ([terms[-1]] if len(terms) % 2 else [])
    return terms[0]


def delay_runs(value, by):
    moved = pltpu.roll(value, by, 0)
    return jnp.where(lax.broadcasted_iota(jnp.int32, value.shape, 0) < by, 0.0, moved)


def operator(spot, *refs):
    piece, pieces, sends, sliced, raw, ahead = spot
    place = lax.axis_index("seq")
    refs = list(refs)
    take = lambda count: [refs.pop(0) for _ in range(count)]
    given, outs = take(6), take(len(sends))
    ahead = take(6) if ahead else []
    if raw:
        held, sem = take(6), take(1)[0]

        def bring(first, into, which):
            column = first * LANES if sliced else (place * pieces + first) * LANES
            own = pl.ds(pl.multiple_of(column, LANES), LANES)
            ids, table, taps, residue, decay, skip = given
            pairs = [(ids, into[0])]
            for k in range(3):
                pairs.append((table.at[k, :, pl.ds(first * LANES, LANES)], into[1].at[:, pl.ds(k * LANES, LANES)]))
            pairs.append((taps.at[:, :, own], into[2]))
            for ref, target in zip((residue, decay, skip), into[3:]):
                pairs.append((ref.at[:, own], target))
            return [pltpu.make_async_copy(x, y, sem.at[which, n]) for n, (x, y) in enumerate(pairs)]

        now = bring(piece, held, 0)
        later = bring(piece + 1, ahead, 1) if ahead else []
        for copy in now + later:
            copy.start()
        for copy in now:
            copy.wait()
    else:
        held, later = given, []
    compute(place, sends, held, outs, *refs)
    for copy in later:
        copy.wait()


def compute(place, sends, held, outs, halo, query, gated, inputs, factors, result, *streams):
    ids, table, taps, residue, decay, skip = held
    length = ids.shape[0] * ids.shape[1]
    steps = length // RUNS
    vocab = table.shape[0]
    width = taps.shape[1]
    modes = residue.shape[0]
    rim = width - 1
    tile = (RUNS, LANES)
    spread = lambda row: jnp.broadcast_to(row, tile)

    cols = ids.shape[1]
    part = cols // len(streams)
    word = lax.broadcasted_iota(jnp.int32, (RUNS, vocab), 1)

    def look_up(here, first, count):
        hot = [
            jnp.where(jnp.broadcast_to(here[:, j : j + 1], word.shape) == word, 1.0, 0.0)
            for j in range(first, first + count)
        ]
        hot = jnp.concatenate(hot, axis=0).astype(jnp.bfloat16)
        found = jnp.dot(hot, table[...], preferred_element_type=jnp.float32)
        return [found[:, k * LANES : (k + 1) * LANES] for k in range(3)]

    def ids_of(block):
        return ids[pl.ds(block, RUNS, stride=steps // cols), :]

    tail = look_up(ids_of(steps // cols - 1), cols - rim, rim)
    for k in range(3):
        for j in range(rim):
            rows = slice(j * RUNS, (j + 1) * RUNS)
            halo[k, rows, :] = delay_runs(tail[k][rows], 1)

    filters = [[spread(taps[k, lag : lag + 1, :]) for lag in range(width)] for k in range(3)]

    def block_step(block, _):
        here = ids_of(block)
        seen = {}

        def row(k, j):
            if (k, j) not in seen:
                if j < 0:
                    seen[k, j] = halo[k, (rim + j) * RUNS : (rim + j + 1) * RUNS, :]
                else:
                    first = j % part * RUNS
                    seen[k, j] = streams[j // part][k, first : first + RUNS, :]
            return seen[k, j]

        def mix(first):
            for j in range(first, first + part):
                mixed = [
                    tree_sum([filters[k][lag] * row(k, j - lag) for lag in range(width)]) for k in range(3)
                ]
                at = pl.ds(pl.multiple_of((block * cols + j) * RUNS, RUNS), RUNS)
                query[at, :] = mixed[0]
                gated[at, :] = mixed[1] * mixed[2]

        for n, stream in enumerate(streams):
            for k, found in enumerate(look_up(here, n * part, part)):
                stream[k] = found
            if n > 0:
                mix((n - 1) * part)
        mix(cols - part)
        for k in range(3):
            halo[k] = streams[-1][k, (part - rim) * RUNS :, :]
        return 0

    lax.fori_loop(0, steps // cols, block_step, 0)

    batch = factors.shape[0] // modes
    rate = decay[...] / length
    weight = residue[...] * jnp.sqrt(2.0 * rate)
    pole = jnp.exp(-rate)
    power = weight
    early = []
    for n in range(batch):
        early.append(spread(jnp.sum(power, axis=0, keepdims=True)))
        power = weight * jnp.exp(-rate * (n + 1))
        for s in range(modes):
            factors[n * modes + s] = spread(power[s : s + 1])
    early[0] = early[0] + spread(skip[...])
    poles = [spread(pole[s : s + 1]) for s in range(modes)]
    leap = jnp.exp(-rate * batch)
    leaps = [spread(leap[s : s + 1]) for s in range(modes)]

    def tokens(ref, m):
        first = m * batch
        return [ref[pl.ds(pl.multiple_of((first + n) * RUNS, RUNS), RUNS), :] for n in range(batch)]

    def advance(m, state):
        values = tokens(gated, m)
        after = []
        for s in range(modes):
            taken = values[0]
            for value in values[1:]:
                taken = poles[s] * taken + value
            inputs[s, pl.ds(pl.multiple_of(m * RUNS, RUNS), RUNS), :] = taken
            after.append(leaps[s] * state[s] + taken)
        return tuple(after)

    zero = jnp.zeros(tile, jnp.float32)
    ends = lax.fori_loop(0, steps // batch, advance, (zero,) * modes, unroll=4)
    begins = []
    for s in range(modes):
        value = delay_runs(ends[s], 1)
        by = 1
        while by < RUNS:
            value = value + spread(jnp.exp(-rate[s : s + 1] * (steps * by))) * delay_runs(value, by)
            by *= 2
        begins.append(value)

    def emit(m, state):
        values = tokens(gated, m)
        for n, asked in enumerate(tokens(query, m)):
            terms = [early[lag] * values[n - lag] for lag in range(n + 1)]
            terms += [factors[n * modes + s] * state[s] for s in range(modes)]
            result[pl.ds(m * batch + n, RUNS, stride=steps), :] = asked * tree_sum(terms)
        at = pl.ds(pl.multiple_of(m * RUNS, RUNS), RUNS)
        return tuple(leaps[s] * state[s] + inputs[s, at, :] for s in range(modes))

    lax.fori_loop(0, steps // batch, emit, tuple(begins), unroll=4)
    for out, hops in zip(outs, sends):
        size = out.shape[0] // len(hops)
        for n, hop in enumerate(hops):
            first = 0 if hop is None else pl.multiple_of(jnp.bitwise_xor(place, hop) * size, size)
            out[n * size : (n + 1) * size, :] = result[pl.ds(first, size), :].astype(jnp.bfloat16)


def run_operator(given, piece, pieces, sends, places, sliced):
    ids, table, taps, residue = given[:4]
    raw = piece == 0 or pieces > 2
    ahead = piece == 0 and pieces == 2
    vocab, modes, width = table.shape[-2], residue.shape[0], taps.shape[1]
    length = ids.size
    steps = length // RUNS
    cols = ids.shape[1]
    parts = max(cols // 32, 1)
    batch = max(4, steps // 128)
    inside = pl.BlockSpec(memory_space=pltpu.VMEM)
    outside = pl.BlockSpec(memory_space=pltpu.HBM)
    floats = lambda *shape: pltpu.VMEM(shape + (LANES,), jnp.float32)
    own = [
        jax.ShapeDtypeStruct(ids.shape, jnp.int32),
        jax.ShapeDtypeStruct((vocab, 3 * LANES), jnp.bfloat16),
        jax.ShapeDtypeStruct((3, width, LANES), jnp.float32),
        jax.ShapeDtypeStruct((modes, LANES), jnp.float32),
        jax.ShapeDtypeStruct((modes, LANES), jnp.float32),
        jax.ShapeDtypeStruct((1, LANES), jnp.float32),
    ]
    rows = [length if hops == [None] else length // places * len(hops) for hops in sends]
    out_shape = [jax.ShapeDtypeStruct((count, LANES), jnp.bfloat16) for count in rows]
    scratch = []
    if raw:
        scratch = [pltpu.VMEM(x.shape, x.dtype) for x in own] + [pltpu.SemaphoreType.DMA((2, 8))]
        out_shape = out_shape + (own if ahead else [])
    scratch += [
        floats(3, (width - 1) * RUNS),
        floats(length),
        floats(length),
        floats(modes, steps // batch * RUNS),
        floats(batch * modes, RUNS),
        floats(length),
    ]
    scratch += [floats(3, cols // parts * RUNS)] * parts
    held = scratch + own * 2 + out_shape
    room = sum(math.prod(x.shape) * jnp.dtype(x.dtype).itemsize for x in held if x.dtype in (jnp.float32, jnp.bfloat16))
    results = pl.pallas_call(
        functools.partial(operator, (piece, pieces, sends, sliced, raw, ahead)),
        in_specs=[outside if raw else inside] * 6,
        out_specs=[inside] * len(out_shape),
        out_shape=out_shape,
        scratch_shapes=scratch,
        compiler_params=pltpu.CompilerParams(vmem_limit_bytes=room + 4 * 2**20),
        cost_estimate=pl.CostEstimate(flops=length * LANES * 8000, bytes_accessed=4 * 2**20, transcendentals=0),
    )(*(given if not raw else [pltpu.with_memory_space_constraint(x, pltpu.HBM) for x in given]))
    return results[: len(sends)], results[len(sends) :]


def run_join(places, blocks, out):
    arrays = [array for array, _ in blocks]
    into = [] if out is None else [out]
    local, kept = arrays[0].shape[-2:]
    count = sum(len(marks) - marks.count(None) for _, marks in blocks)

    def kernel(*refs):
        refs = list(refs)
        if into:
            refs.pop(len(arrays))
        *refs, out, sem = refs
        place = lax.axis_index("seq")
        copies = []
        for ref, (_, marks) in zip(refs, blocks):
            for n, mark in enumerate(marks):
                if mark is None:
                    continue
                piece, hop, *plain = mark
                first = ((hop if plain else jnp.bitwise_xor(place, hop)) * 2 + piece) * kept
                target = out.at[:, pl.ds(first if plain else pl.multiple_of(first, kept), kept)]
                copies.append(pltpu.make_async_copy(ref.at[n], target, sem.at[len(copies)]))
        for copy in copies:
            copy.start()
        for copy in copies:
            copy.wait()

    anywhere = pl.BlockSpec(memory_space=pl.ANY)
    return pl.pallas_call(
        kernel,
        in_specs=[anywhere] * (len(arrays) + len(into)),
        out_specs=anywhere,
        out_shape=jax.ShapeDtypeStruct((local, places * 2 * kept), arrays[0].dtype),
        scratch_shapes=[pltpu.SemaphoreType.DMA((count,))],
        input_output_aliases={len(arrays): 0} if into else {},
        compiler_params=pltpu.CompilerParams(vmem_limit_bytes=2**20),
    )(*(pltpu.with_memory_space_constraint(x, pltpu.VMEM) for x in arrays), *into)


def by_hops(given, places, local):
    far = list(range(0, places, 4))
    hop = lambda x, by: lax.ppermute(x, "seq", [(i, i ^ by) for i in range(places)])

    def run(given, piece, sends):
        results, ahead = run_operator(given, piece, 2, sends, places, False)
        return [x.reshape(-1, local, x.shape[-1]) for x in results], ahead

    first, given = run(given, 0, [[d + e for e in range(4)] for d in far])
    landed = first[:1] + [hop(x, d) for x, d in zip(first[1:], far[1:])]
    (*straight, across), _ = run(given, 1, [[d, d + 1] for d in far] + [[d + e for d in far for e in (2, 3)]])
    landed, straight = lax.optimization_barrier((landed, straight))
    crossed = hop(across, 2)
    final = [
        hop(jnp.concatenate([straight[n], crossed[2 * n : 2 * n + 2]]), d) for n, d in enumerate(far) if d > 0
    ]
    turned = hop(jnp.concatenate([x[2:] for x in landed]), 2)
    odd = [x[1:2] for x in landed] + [turned[2 * n + 1 : 2 * n + 2] for n in range(len(far))]
    out = run_join(
        places,
        [(x, [(0, d)]) for x, d in zip(landed, far)]
        + [(turned, [mark for d in far for mark in ((0, d + 2), None)])]
        + [(hop(jnp.concatenate(odd), 1), [(0, d + 1) for d in far] + [(0, d + 3) for d in far])],
        None,
    )
    odd = [straight[0][1:2], crossed[1:2]] + [x[n : n + 1] for x in final for n in (1, 3)]
    return run_join(
        places,
        [(straight[0], [(1, 0)]), (crossed, [(1, 2)])]
        + [(x, [(1, d), None, (1, d + 2)]) for x, d in zip(final, far[1:])]
        + [(hop(jnp.concatenate(odd), 1), [(1, d + e) for d in far for e in (1, 3)])],
        out,
    )


def body(token_ids, vocab_table, short_filter, residue, decay, skip_gain):
    places = lax.axis_size("seq")
    place = lax.axis_index("seq")
    length = token_ids.shape[0]
    local = length // places
    share = vocab_table.shape[2]
    pieces = -(-share // LANES)
    ids = token_ids.reshape(-1, min(LANES, length // RUNS))
    table = vocab_table.transpose(1, 0, 2)
    rows = [short_filter.transpose(1, 0, 2), residue.T, decay.T, skip_gain[None]]
    sliced = share % LANES != 0
    if sliced:
        widen = lambda x: jnp.pad(x, [(0, 0)] * (x.ndim - 1) + [(0, pieces * LANES - share)])
        rows = [widen(lax.dynamic_slice_in_dim(x, place * share, share, x.ndim - 1)) for x in rows]
        table = widen(table)
    given = (ids, table, *rows)
    if not sliced and pieces == 2 and places % 4 == 0 and places & (places - 1) == 0 and places > 4:
        return by_hops(given, places, local)
    parts = []
    for piece in range(pieces):
        blocks, ahead = run_operator(given, piece, pieces, [[None]], places, sliced)
        given = ahead or given
        kept = min(LANES, share - piece * LANES)
        sent = blocks[0][:, :kept].reshape(places, local, kept)
        parts.append(lax.all_to_all(sent, "seq", split_axis=0, concat_axis=0, tiled=True))
    return jnp.concatenate(parts, axis=2).transpose(1, 0, 2).reshape(local, places * share)


def solution(mesh):
    placed = (P("groups"), P(None, None, "seq"), P(), P(), P(), P())
    return jax.shard_map(
        body, mesh=mesh, in_specs=placed, out_specs=P(("groups", "seq"), None), check_vma=False
    )
```

```python
import functools
import math

import jax
import jax.numpy as jnp
from jax import lax
from jax.experimental import pallas as pl
from jax.experimental.pallas import tpu as pltpu
from jax.sharding import PartitionSpec as P

LANES = 128
RUNS = 8


def tree_sum(terms):
    while len(terms) > 1:
        pairs = [a + b for a, b in zip(terms[::2], terms[1::2])]
        terms = pairs + ([terms[-1]] if len(terms) % 2 else [])
    return terms[0]


def delay_runs(value, by):
    moved = pltpu.roll(value, by, 0)
    return jnp.where(lax.broadcasted_iota(jnp.int32, value.shape, 0) < by, 0.0, moved)


def operator(spot, *refs):
    piece, pieces, sends, sliced, raw, ahead = spot
    place = lax.axis_index("seq")
    refs = list(refs)
    take = lambda count: [refs.pop(0) for _ in range(count)]
    given, outs = take(6), take(len(sends))
    ahead = take(6) if ahead else []
    if raw:
        held, sem = take(6), take(1)[0]

        def bring(first, into, which):
            column = first * LANES if sliced else (place * pieces + first) * LANES
            own = pl.ds(pl.multiple_of(column, LANES), LANES)
            ids, table, taps, residue, decay, skip = given
            pairs = [(ids, into[0])]
            half = into[1].shape[0]
            for n in range(6):
                words, column = pl.ds(n // 3 * half, half), pl.ds(first * LANES, LANES)
                pairs.append((table.at[n % 3, words, column], into[1].at[:, pl.ds(n * LANES, LANES)]))
            pairs.append((taps.at[:, :, own], into[2]))
            for ref, target in zip((residue, decay, skip), into[3:]):
                pairs.append((ref.at[:, own], target))
            return [pltpu.make_async_copy(x, y, sem.at[which, n]) for n, (x, y) in enumerate(pairs)]

        now = bring(piece, held, 0)
        later = bring(piece + 1, ahead, 1) if ahead else []
        for copy in now + later:
            copy.start()
        for copy in now:
            copy.wait()
    else:
        held, later = given, []
    compute(place, sends, held, outs, *refs)
    for copy in later:
        copy.wait()


def compute(place, sends, held, outs, halo, query, gated, inputs, result, *streams):
    ids, table, taps, residue, decay, skip = held
    length = ids.shape[0] * ids.shape[1]
    steps = length // RUNS
    half = table.shape[0]
    width = taps.shape[1]
    modes = residue.shape[0]
    rim = width - 1
    tile = (RUNS, LANES)
    spread = lambda row: jnp.broadcast_to(row, tile)

    cols = ids.shape[1]
    part = cols // len(streams)
    word = lax.broadcasted_iota(jnp.int32, (RUNS, half), 1)

    def look_up(here, first, count, place_row):
        upper = here >= half
        within = jnp.where(upper, here - half, here)
        hot = [
            jnp.where(jnp.broadcast_to(within[:, j : j + 1], word.shape) == word, 1.0, 0.0)
            for j in range(first, first + count)
        ]
        hot = jnp.concatenate(hot, axis=0).astype(jnp.bfloat16)
        found = jnp.dot(hot, table[...], preferred_element_type=jnp.float32)
        for j in range(count):
            above = spread(here[:, first + j : first + j + 1]) >= half
            rows = found[j * RUNS : (j + 1) * RUNS]
            for k in range(3):
                low, high = (rows[:, n * LANES : (n + 1) * LANES] for n in (k, k + 3))
                place_row(k, j, jnp.where(above, high, low))

    def ids_of(block):
        return ids[pl.ds(block, RUNS, stride=steps // cols), :]

    def place_tail(k, j, row):
        halo[k, j * RUNS : (j + 1) * RUNS, :] = delay_runs(row, 1)

    look_up(ids_of(steps // cols - 1), cols - rim, rim, place_tail)

    filters = [[spread(taps[k, lag : lag + 1, :]) for lag in range(width)] for k in range(3)]

    def block_step(block, _):
        here = ids_of(block)
        seen = {}

        def row(k, j):
            if (k, j) not in seen:
                if j < 0:
                    seen[k, j] = halo[k, (rim + j) * RUNS : (rim + j + 1) * RUNS, :]
                else:
                    first = j % part * RUNS
                    seen[k, j] = streams[j // part][k, first : first + RUNS, :]
            return seen[k, j]

        def mix(first):
            for j in range(first, first + part):
                mixed = [
                    tree_sum([filters[k][lag] * row(k, j - lag) for lag in range(width)]) for k in range(3)
                ]
                at = pl.ds(pl.multiple_of((block * cols + j) * RUNS, RUNS), RUNS)
                query[at, :] = mixed[0]
                gated[at, :] = mixed[1] * mixed[2]

        for n, stream in enumerate(streams):

            def place_row(k, j, row, stream=stream):
                stream[k, j * RUNS : (j + 1) * RUNS, :] = row

            look_up(here, n * part, part, place_row)
            if n > 0:
                mix((n - 1) * part)
        mix(cols - part)
        for k in range(3):
            halo[k] = streams[-1][k, (part - rim) * RUNS :, :]
        return 0

    lax.fori_loop(0, steps // cols, block_step, 0)

    batch = steps // inputs.shape[0]
    rate = decay[...] / length
    weight = residue[...] * jnp.sqrt(2.0 * rate)
    pole = jnp.exp(-rate)
    power = weight
    early = []
    for n in range(batch):
        early.append(spread(jnp.sum(power, axis=0, keepdims=True)))
        power = weight * jnp.exp(-rate * (n + 1))
    early[0] = early[0] + spread(skip[...])
    poles = [spread(pole[s : s + 1]) for s in range(modes)]
    leap = jnp.exp(-rate * batch)
    leaps = [spread(leap[s : s + 1]) for s in range(modes)]

    def tokens(ref, m):
        first = m * batch
        return [ref[pl.ds(pl.multiple_of((first + n) * RUNS, RUNS), RUNS), :] for n in range(batch)]

    def advance(m, state):
        values = tokens(gated, m)
        after = []
        for s in range(modes):
            taken = values[0]
            for value in values[1:]:
                taken = poles[s] * taken + value
            inputs[m, s * RUNS : (s + 1) * RUNS, :] = taken
            after.append(leaps[s] * state[s] + taken)
        return tuple(after)

    zero = jnp.zeros(tile, jnp.float32)
    ends = lax.fori_loop(0, steps // batch, advance, (zero,) * modes, unroll=4)
    begins = []
    for s in range(modes):
        value = delay_runs(ends[s], 1)
        by = 1
        while by < RUNS:
            value = value + spread(jnp.exp(-rate[s : s + 1] * (steps * by))) * delay_runs(value, by)
            by *= 2
        begins.append(value)

    weights = [spread(weight[s : s + 1]) for s in range(modes)]

    def emit(m, terms):
        values = tokens(gated, m)
        answers = []
        for n, asked in enumerate(tokens(query, m)):
            terms = [p * x for p, x in zip(poles, terms)]
            close = [early[lag] * values[n - lag] for lag in range(n + 1)]
            answers.append(asked * tree_sum(close + terms))
        for n, answer in enumerate(answers):
            result[pl.ds(m * batch + n, RUNS, stride=steps), :] = answer
        return tuple(x + w * inputs[m, s * RUNS : (s + 1) * RUNS, :] for s, (w, x) in enumerate(zip(weights, terms)))

    lax.fori_loop(0, steps // batch, emit, tuple(w * x for w, x in zip(weights, begins)), unroll=4)
    for out, hops in zip(outs, sends):
        size = out.shape[0] // len(hops)
        for n, hop in enumerate(hops):
            first = 0 if hop is None else pl.multiple_of(jnp.bitwise_xor(place, hop) * size, size)
            out[n * size : (n + 1) * size, :] = result[pl.ds(first, size), :].astype(jnp.bfloat16)


def run_operator(given, piece, pieces, sends, places, sliced):
    ids, table, taps, residue = given[:4]
    raw = piece == 0 or pieces > 2
    ahead = piece == 0 and pieces == 2
    vocab, modes, width = table.shape[-2], residue.shape[0], taps.shape[1]
    length = ids.size
    steps = length // RUNS
    cols = ids.shape[1]
    parts = max(cols // 32, 1)
    batch = max(4, steps // 128)
    inside = pl.BlockSpec(memory_space=pltpu.VMEM)
    outside = pl.BlockSpec(memory_space=pltpu.HBM)
    floats = lambda *shape: pltpu.VMEM(shape + (LANES,), jnp.float32)
    own = [
        jax.ShapeDtypeStruct(ids.shape, jnp.int32),
        jax.ShapeDtypeStruct((vocab // 2, 6 * LANES), jnp.bfloat16),
        jax.ShapeDtypeStruct((3, width, LANES), jnp.float32),
        jax.ShapeDtypeStruct((modes, LANES), jnp.float32),
        jax.ShapeDtypeStruct((modes, LANES), jnp.float32),
        jax.ShapeDtypeStruct((1, LANES), jnp.float32),
    ]
    rows = [length if hops == [None] else length // places * len(hops) for hops in sends]
    out_shape = [jax.ShapeDtypeStruct((count, LANES), jnp.bfloat16) for count in rows]
    scratch = []
    if raw:
        scratch = [pltpu.VMEM(x.shape, x.dtype) for x in own] + [pltpu.SemaphoreType.DMA((2, 11))]
        out_shape = out_shape + (own if ahead else [])
    scratch += [
        floats(3, (width - 1) * RUNS),
        floats(length),
        floats(length),
        floats(steps // batch, modes * RUNS),
        floats(length),
    ]
    scratch += [floats(3, cols // parts * RUNS)] * parts
    held = scratch + own * 2 + out_shape
    room = sum(math.prod(x.shape) * jnp.dtype(x.dtype).itemsize for x in held if x.dtype in (jnp.float32, jnp.bfloat16))
    results = pl.pallas_call(
        functools.partial(operator, (piece, pieces, sends, sliced, raw, ahead)),
        in_specs=[outside if raw else inside] * 6,
        out_specs=[inside] * len(out_shape),
        out_shape=out_shape,
        scratch_shapes=scratch,
        compiler_params=pltpu.CompilerParams(vmem_limit_bytes=room + 4 * 2**20),
        cost_estimate=pl.CostEstimate(flops=length * LANES * 8000, bytes_accessed=4 * 2**20, transcendentals=0),
    )(*(given if not raw else [pltpu.with_memory_space_constraint(x, pltpu.HBM) for x in given]))
    return results[: len(sends)], results[len(sends) :]


def run_join(places, blocks, out):
    arrays = [array for array, _ in blocks]
    into = [] if out is None else [out]
    local, kept = arrays[0].shape[-2:]
    count = sum(len(marks) - marks.count(None) for _, marks in blocks)

    def kernel(*refs):
        refs = list(refs)
        if into:
            refs.pop(len(arrays))
        *refs, out, sem = refs
        place = lax.axis_index("seq")
        copies = []
        for ref, (_, marks) in zip(refs, blocks):
            for n, mark in enumerate(marks):
                if mark is None:
                    continue
                piece, hop, *plain = mark
                first = ((hop if plain else jnp.bitwise_xor(place, hop)) * 2 + piece) * kept
                target = out.at[:, pl.ds(first if plain else pl.multiple_of(first, kept), kept)]
                copies.append(pltpu.make_async_copy(ref.at[n], target, sem.at[len(copies)]))
        for copy in copies:
            copy.start()
        for copy in copies:
            copy.wait()

    anywhere = pl.BlockSpec(memory_space=pl.ANY)
    return pl.pallas_call(
        kernel,
        in_specs=[anywhere] * (len(arrays) + len(into)),
        out_specs=anywhere,
        out_shape=jax.ShapeDtypeStruct((local, places * 2 * kept), arrays[0].dtype),
        scratch_shapes=[pltpu.SemaphoreType.DMA((count,))],
        input_output_aliases={len(arrays): 0} if into else {},
        cost_estimate=pl.CostEstimate(flops=0, bytes_accessed=2**23, transcendentals=0),
        compiler_params=pltpu.CompilerParams(vmem_limit_bytes=2**20),
    )(*(pltpu.with_memory_space_constraint(x, pltpu.VMEM) for x in arrays), *into)


def by_hops(given, places, local):
    far = list(range(0, places, 4))
    hop = lambda x, by: lax.ppermute(x, "seq", [(i, i ^ by) for i in range(places)])

    def run(given, piece, sends):
        results, ahead = run_operator(given, piece, 2, sends, places, False)
        return [x.reshape(-1, local, x.shape[-1]) for x in results], ahead

    first, given = run(given, 0, [[d + e for e in range(4)] for d in far])
    landed = first[:1] + [hop(x, d) for x, d in zip(first[1:], far[1:])]
    sends = [[d, d + 1] for d in far] + [[d + e for d in far[1:] for e in (2, 3)], [2, 3]]
    (*straight, across, beside), _ = run(given, 1, sends)
    landed, straight = lax.optimization_barrier((landed, straight))
    crossed = hop(across, 2)
    final = [hop(jnp.concatenate([straight[n], crossed[2 * n - 2 : 2 * n]]), far[n]) for n in range(1, len(far))]
    turn = jnp.concatenate([x[2:] for x in landed] + [beside])
    turn, crossed = lax.optimization_barrier((turn, crossed))
    turned = hop(turn, 2)
    paired = hop(jnp.concatenate([straight[0][1:2]] + [x[n : n + 1] for x in final for n in (1, 3)]), 1)
    out = run_join(
        places,
        [(straight[0], [(1, 0)])] + [(x, [(1, d), None, (1, d + 2)]) for x, d in zip(final, far[1:])],
        None,
    )
    odd = [x[1:2] for x in landed] + [turned[n : n + 1] for n in range(1, turn.shape[0], 2)]
    return run_join(
        places,
        [(x, [(0, d)]) for x, d in zip(landed, far)]
        + [(turned, [mark for d in far for mark in ((0, d + 2), None)] + [(1, 2)])]
        + [(paired, [(1, 1)] + [(1, d + e) for d in far[1:] for e in (1, 3)])]
        + [(hop(jnp.concatenate(odd), 1), [(0, d + 1) for d in far] + [(0, d + 3) for d in far] + [(1, 3)])],
        out,
    )


def body(token_ids, vocab_table, short_filter, residue, decay, skip_gain):
    places = lax.axis_size("seq")
    place = lax.axis_index("seq")
    length = token_ids.shape[0]
    local = length // places
    share = vocab_table.shape[2]
    pieces = -(-share // LANES)
    ids = token_ids.reshape(-1, min(LANES, length // RUNS))
    table = vocab_table.transpose(1, 0, 2)
    rows = [short_filter.transpose(1, 0, 2), residue.T, decay.T, skip_gain[None]]
    sliced = share % LANES != 0
    if sliced:
        widen = lambda x: jnp.pad(x, [(0, 0)] * (x.ndim - 1) + [(0, pieces * LANES - share)])
        rows = [widen(lax.dynamic_slice_in_dim(x, place * share, share, x.ndim - 1)) for x in rows]
        table = widen(table)
    given = (ids, table, *rows)
    if not sliced and pieces == 2 and places % 4 == 0 and places & (places - 1) == 0 and places > 4:
        return by_hops(given, places, local)
    parts = []
    for piece in range(pieces):
        blocks, ahead = run_operator(given, piece, pieces, [[None]], places, sliced)
        given = ahead or given
        kept = min(LANES, share - piece * LANES)
        sent = blocks[0][:, :kept].reshape(places, local, kept)
        parts.append(lax.all_to_all(sent, "seq", split_axis=0, concat_axis=0, tiled=True))
    return jnp.concatenate(parts, axis=2).transpose(1, 0, 2).reshape(local, places * share)


def solution(mesh):
    placed = (P("groups"), P(None, None, "seq"), P(), P(), P(), P())
    return jax.shard_map(
        body, mesh=mesh, in_specs=placed, out_specs=P(("groups", "seq"), None), check_vma=False
    )
```

```python
import functools
import math

import jax
import jax.numpy as jnp
from jax import lax
from jax.experimental import pallas as pl
from jax.experimental.pallas import tpu as pltpu
from jax.sharding import PartitionSpec as P

LANES = 128
RUNS = 8


def tree_sum(terms):
    while len(terms) > 1:
        pairs = [a + b for a, b in zip(terms[::2], terms[1::2])]
        terms = pairs + ([terms[-1]] if len(terms) % 2 else [])
    return terms[0]


def delay_runs(value, by):
    moved = pltpu.roll(value, by, 0)
    return jnp.where(lax.broadcasted_iota(jnp.int32, value.shape, 0) < by, 0.0, moved)


def operator(spot, *refs):
    piece, pieces, sends, sliced, raw, ahead = spot
    place = lax.axis_index("seq")
    refs = list(refs)
    take = lambda count: [refs.pop(0) for _ in range(count)]
    given, outs = take(6), take(len(sends))
    ahead = take(6) if ahead else []
    if raw:
        held, sem = take(6), take(1)[0]

        def bring(first, into, which):
            column = first * LANES if sliced else (place * pieces + first) * LANES
            own = pl.ds(pl.multiple_of(column, LANES), LANES)
            ids, table, taps, residue, decay, skip = given
            pairs = [(ids, into[0])]
            half = into[1].shape[0]
            for n in range(6):
                words, column = pl.ds(n // 3 * half, half), pl.ds(first * LANES, LANES)
                pairs.append((table.at[n % 3, words, column], into[1].at[:, pl.ds(n * LANES, LANES)]))
            pairs.append((taps.at[:, :, own], into[2]))
            for ref, target in zip((residue, decay, skip), into[3:]):
                pairs.append((ref.at[:, own], target))
            return [pltpu.make_async_copy(x, y, sem.at[which, n]) for n, (x, y) in enumerate(pairs)]

        now = bring(piece, held, 0)
        later = bring(piece + 1, ahead, 1) if ahead else []
        for copy in now:
            copy.start()
        for copy in now:
            copy.wait()
        for copy in later:
            copy.start()
    else:
        held, later = given, []
    compute(place, sends, held, outs, *refs)
    for copy in later:
        copy.wait()


def compute(place, sends, held, outs, halo, query, gated, inputs, gains, result, *streams):
    ids, table, taps, residue, decay, skip = held
    length = ids.shape[0] * ids.shape[1]
    steps = length // RUNS
    half = table.shape[0]
    width = taps.shape[1]
    modes = residue.shape[0]
    rim = width - 1
    tile = (RUNS, LANES)
    spread = lambda row: jnp.broadcast_to(row, tile)

    cols = ids.shape[1]
    part = cols // len(streams)
    word = lax.broadcasted_iota(jnp.int32, (RUNS, half), 1)

    def look_up(here, first, count, place_row):
        upper = here >= half
        within = jnp.where(upper, here - half, here)
        hot = [
            jnp.where(jnp.broadcast_to(within[:, j : j + 1], word.shape) == word, 1.0, 0.0)
            for j in range(first, first + count)
        ]
        hot = jnp.concatenate(hot, axis=0).astype(jnp.bfloat16)
        found = jnp.dot(hot, table[...], preferred_element_type=jnp.float32)
        for j in range(count):
            above = spread(here[:, first + j : first + j + 1]) >= half
            rows = found[j * RUNS : (j + 1) * RUNS]
            for k in range(3):
                low, high = (rows[:, n * LANES : (n + 1) * LANES] for n in (k, k + 3))
                place_row(k, j, jnp.where(above, high, low))

    def ids_of(block):
        return ids[pl.ds(block, RUNS, stride=steps // cols), :]

    def place_tail(k, j, row):
        halo[k, j * RUNS : (j + 1) * RUNS, :] = delay_runs(row, 1)

    look_up(ids_of(steps // cols - 1), cols - rim, rim, place_tail)

    filters = [[spread(taps[k, lag : lag + 1, :]) for lag in range(width)] for k in range(3)]

    def block_step(block, _):
        here = ids_of(block)
        seen = {}

        def row(k, j):
            if (k, j) not in seen:
                if j < 0:
                    seen[k, j] = halo[k, (rim + j) * RUNS : (rim + j + 1) * RUNS, :]
                else:
                    first = j % part * RUNS
                    seen[k, j] = streams[j // part][k, first : first + RUNS, :]
            return seen[k, j]

        def mix(first):
            for j in range(first, first + part):
                mixed = [
                    tree_sum([filters[k][lag] * row(k, j - lag) for lag in range(width)]) for k in range(3)
                ]
                at = pl.ds(pl.multiple_of((block * cols + j) * RUNS, RUNS), RUNS)
                query[at, :] = mixed[0]
                gated[at, :] = mixed[1] * mixed[2]

        for n, stream in enumerate(streams):

            def place_row(k, j, row, stream=stream):
                stream[k, j * RUNS : (j + 1) * RUNS, :] = row

            look_up(here, n * part, part, place_row)
            if n > 0:
                mix((n - 1) * part)
        mix(cols - part)
        for k in range(3):
            halo[k] = streams[-1][k, (part - rim) * RUNS :, :]
        return 0

    lax.fori_loop(0, steps // cols, block_step, 0)

    batch = steps // inputs.shape[0]
    unroll = max(32 // batch, 1)
    rate = decay[...] / length
    weight = residue[...] * jnp.sqrt(2.0 * rate)
    pole = jnp.exp(-rate)
    power = weight
    early = []
    for n in range(batch):
        early.append(spread(jnp.sum(power, axis=0, keepdims=True)))
        power = weight * jnp.exp(-rate * (n + 1))
    early[0] = early[0] + spread(skip[...])
    poles = [spread(pole[s : s + 1]) for s in range(modes)]
    leap = jnp.exp(-rate * batch)
    leaps = [spread(leap[s : s + 1]) for s in range(modes)]

    def tokens(ref, m):
        first = m * batch
        return [ref[pl.ds(pl.multiple_of((first + n) * RUNS, RUNS), RUNS), :] for n in range(batch)]

    def advance(m, state):
        values = tokens(gated, m)
        after = []
        for s in range(modes):
            taken = values[0]
            for value in values[1:]:
                taken = poles[s] * taken + value
            inputs[m, s * RUNS : (s + 1) * RUNS, :] = taken
            after.append(leaps[s] * state[s] + taken)
        return tuple(after)

    zero = jnp.zeros(tile, jnp.float32)
    ends = lax.fori_loop(0, steps // batch, advance, (zero,) * modes, unroll=unroll)
    begins = []
    for s in range(modes):
        value = delay_runs(ends[s], 1)
        by = 1
        while by < RUNS:
            value = value + spread(jnp.exp(-rate[s : s + 1] * (steps * by))) * delay_runs(value, by)
            by *= 2
        begins.append(value)

    weights = [spread(weight[s : s + 1]) for s in range(modes)]
    for s in range(modes):
        gains[s] = weights[s]

    def emit(m, terms):
        values = tokens(gated, m)
        answers = []
        for n, asked in enumerate(tokens(query, m)):
            terms = [p * x for p, x in zip(poles, terms)]
            close = [early[lag] * values[n - lag] for lag in range(n + 1)]
            answers.append(asked * tree_sum(close + terms))
        for n, answer in enumerate(answers):
            result[pl.ds(m * batch + n, RUNS, stride=steps), :] = answer
        return tuple(x + gains[s] * inputs[m, s * RUNS : (s + 1) * RUNS, :] for s, x in enumerate(terms))

    lax.fori_loop(0, steps // batch, emit, tuple(w * x for w, x in zip(weights, begins)), unroll=unroll)
    for out, hops in zip(outs, sends):
        size = out.shape[0] // len(hops)
        for n, hop in enumerate(hops):
            first = 0 if hop is None else pl.multiple_of(jnp.bitwise_xor(place, hop) * size, size)
            out[n * size : (n + 1) * size, :] = result[pl.ds(first, size), :].astype(jnp.bfloat16)


def run_operator(given, piece, pieces, sends, places, sliced):
    ids, table, taps, residue = given[:4]
    raw = piece == 0 or pieces > 2
    ahead = piece == 0 and pieces == 2
    vocab, modes, width = table.shape[-2], residue.shape[0], taps.shape[1]
    length = ids.size
    steps = length // RUNS
    cols = ids.shape[1]
    parts = max(cols // 32, 1)
    batch = max(4, steps // 128)
    inside = pl.BlockSpec(memory_space=pltpu.VMEM)
    outside = pl.BlockSpec(memory_space=pltpu.HBM)
    floats = lambda *shape: pltpu.VMEM(shape + (LANES,), jnp.float32)
    own = [
        jax.ShapeDtypeStruct(ids.shape, jnp.int32),
        jax.ShapeDtypeStruct((vocab // 2, 6 * LANES), jnp.bfloat16),
        jax.ShapeDtypeStruct((3, width, LANES), jnp.float32),
        jax.ShapeDtypeStruct((modes, LANES), jnp.float32),
        jax.ShapeDtypeStruct((modes, LANES), jnp.float32),
        jax.ShapeDtypeStruct((1, LANES), jnp.float32),
    ]
    rows = [length if hops == [None] else length // places * len(hops) for hops in sends]
    out_shape = [jax.ShapeDtypeStruct((count, LANES), jnp.bfloat16) for count in rows]
    scratch = []
    if raw:
        scratch = [pltpu.VMEM(x.shape, x.dtype) for x in own] + [pltpu.SemaphoreType.DMA((2, 11))]
        out_shape = out_shape + (own if ahead else [])
    scratch += [
        floats(3, (width - 1) * RUNS),
        floats(length),
        floats(length),
        floats(steps // batch, modes * RUNS),
        floats(modes, RUNS),
        floats(length),
    ]
    scratch += [floats(3, cols // parts * RUNS)] * parts
    held = scratch + own * 2 + out_shape
    room = sum(math.prod(x.shape) * jnp.dtype(x.dtype).itemsize for x in held if x.dtype in (jnp.float32, jnp.bfloat16))
    results = pl.pallas_call(
        functools.partial(operator, (piece, pieces, sends, sliced, raw, ahead)),
        in_specs=[outside if raw else inside] * 6,
        out_specs=[inside] * len(out_shape),
        out_shape=out_shape,
        scratch_shapes=scratch,
        compiler_params=pltpu.CompilerParams(vmem_limit_bytes=room + 4 * 2**20),
        cost_estimate=pl.CostEstimate(flops=length * LANES * 8000, bytes_accessed=4 * 2**20, transcendentals=0),
    )(*(given if not raw else [pltpu.with_memory_space_constraint(x, pltpu.HBM) for x in given]))
    return results[: len(sends)], results[len(sends) :]


def run_join(places, blocks, out):
    arrays = [array for array, _ in blocks]
    into = [] if out is None else [out]
    local, kept = arrays[0].shape[-2:]
    count = sum(len(marks) - marks.count(None) for _, marks in blocks)

    def kernel(*refs):
        refs = list(refs)
        if into:
            refs.pop(len(arrays))
        *refs, out, sem = refs
        place = lax.axis_index("seq")
        copies = []
        for ref, (_, marks) in zip(refs, blocks):
            for n, mark in enumerate(marks):
                if mark is None:
                    continue
                piece, hop, *plain = mark
                first = ((hop if plain else jnp.bitwise_xor(place, hop)) * 2 + piece) * kept
                target = out.at[:, pl.ds(first if plain else pl.multiple_of(first, kept), kept)]
                copies.append(pltpu.make_async_copy(ref.at[n], target, sem.at[len(copies)]))
        for copy in copies:
            copy.start()
        for copy in copies:
            copy.wait()

    anywhere = pl.BlockSpec(memory_space=pl.ANY)
    return pl.pallas_call(
        kernel,
        in_specs=[anywhere] * (len(arrays) + len(into)),
        out_specs=anywhere,
        out_shape=jax.ShapeDtypeStruct((local, places * 2 * kept), arrays[0].dtype),
        scratch_shapes=[pltpu.SemaphoreType.DMA((count,))],
        input_output_aliases={len(arrays): 0} if into else {},
        cost_estimate=pl.CostEstimate(flops=0, bytes_accessed=2**23, transcendentals=0),
        compiler_params=pltpu.CompilerParams(vmem_limit_bytes=2**20),
    )(*(pltpu.with_memory_space_constraint(x, pltpu.VMEM) for x in arrays), *into)


def by_hops(given, places, local):
    far = list(range(0, places, 4))
    hop = lambda x, by: lax.ppermute(x, "seq", [(i, i ^ by) for i in range(places)])

    def run(given, piece, sends):
        results, ahead = run_operator(given, piece, 2, sends, places, False)
        return [x.reshape(-1, local, x.shape[-1]) for x in results], ahead

    first, given = run(given, 0, [[d + e for e in range(4)] for d in far])
    landed = [hop(x, d) for x, d in zip(first[:0:-1], far[:0:-1])]
    landed = first[:1] + landed[::-1]
    sends = [[d, d + 1] for d in far] + [[d + e for d in far[1:] for e in (2, 3)], [2, 3]]
    (*straight, across, beside), _ = run(given, 1, sends)
    landed, straight = lax.optimization_barrier((landed, straight))
    crossed = hop(across, 2)
    final = [
        hop(jnp.concatenate([straight[n], crossed[2 * n - 2 : 2 * n]]), far[n]) for n in range(len(far) - 1, 0, -1)
    ][::-1]
    turn = jnp.concatenate([x[2:] for x in landed] + [beside])
    turn, crossed = lax.optimization_barrier((turn, crossed))
    turned = hop(turn, 2)
    paired = hop(jnp.concatenate([straight[0][1:2]] + [x[n : n + 1] for x in final for n in (1, 3)]), 1)
    out = run_join(
        places,
        [(straight[0], [(1, 0)])] + [(x, [(1, d), None, (1, d + 2)]) for x, d in zip(final, far[1:])],
        None,
    )
    odd = [x[1:2] for x in landed] + [turned[n : n + 1] for n in range(1, turn.shape[0], 2)]
    return run_join(
        places,
        [(x, [(0, d)]) for x, d in zip(landed, far)]
        + [(turned, [mark for d in far for mark in ((0, d + 2), None)] + [(1, 2)])]
        + [(paired, [(1, 1)] + [(1, d + e) for d in far[1:] for e in (1, 3)])]
        + [(hop(jnp.concatenate(odd), 1), [(0, d + 1) for d in far] + [(0, d + 3) for d in far] + [(1, 3)])],
        out,
    )


def body(token_ids, vocab_table, short_filter, residue, decay, skip_gain):
    places = lax.axis_size("seq")
    place = lax.axis_index("seq")
    length = token_ids.shape[0]
    local = length // places
    share = vocab_table.shape[2]
    pieces = -(-share // LANES)
    ids = token_ids.reshape(-1, min(LANES, length // RUNS))
    table = vocab_table.transpose(1, 0, 2)
    rows = [short_filter.transpose(1, 0, 2), residue.T, decay.T, skip_gain[None]]
    sliced = share % LANES != 0
    if sliced:
        widen = lambda x: jnp.pad(x, [(0, 0)] * (x.ndim - 1) + [(0, pieces * LANES - share)])
        rows = [widen(lax.dynamic_slice_in_dim(x, place * share, share, x.ndim - 1)) for x in rows]
        table = widen(table)
    given = (ids, table, *rows)
    if not sliced and pieces == 2 and places % 4 == 0 and places & (places - 1) == 0 and places > 4:
        return by_hops(given, places, local)
    parts = []
    for piece in range(pieces):
        blocks, ahead = run_operator(given, piece, pieces, [[None]], places, sliced)
        given = ahead or given
        kept = min(LANES, share - piece * LANES)
        sent = blocks[0][:, :kept].reshape(places, local, kept)
        parts.append(lax.all_to_all(sent, "seq", split_axis=0, concat_axis=0, tiled=True))
    return jnp.concatenate(parts, axis=2).transpose(1, 0, 2).reshape(local, places * share)


def solution(mesh):
    placed = (P("groups"), P(None, None, "seq"), P(), P(), P(), P())
    return jax.shard_map(
        body, mesh=mesh, in_specs=placed, out_specs=P(("groups", "seq"), None), check_vma=False
    )
```

```python
import functools
import math

import jax
import jax.numpy as jnp
from jax import lax
from jax.experimental import pallas as pl
from jax.experimental.pallas import tpu as pltpu
from jax.sharding import PartitionSpec as P

LANES = 128
RUNS = 8


def tree_sum(terms):
    while len(terms) > 1:
        pairs = [a + b for a, b in zip(terms[::2], terms[1::2])]
        terms = pairs + ([terms[-1]] if len(terms) % 2 else [])
    return terms[0]


def delay_runs(value, by):
    moved = pltpu.roll(value, by, 0)
    return jnp.where(lax.broadcasted_iota(jnp.int32, value.shape, 0) < by, 0.0, moved)


def operator(spot, *refs):
    piece, pieces, sends, sliced, raw, ahead = spot
    place = lax.axis_index("seq")
    refs = list(refs)
    take = lambda count: [refs.pop(0) for _ in range(count)]
    given, outs = take(6), take(len(sends))
    ahead = take(6) if ahead else []
    if raw:
        held, sem = take(6), take(1)[0]

        def bring(first, into, which):
            column = first * LANES if sliced else (place * pieces + first) * LANES
            own = pl.ds(pl.multiple_of(column, LANES), LANES)
            ids, table, taps, residue, decay, skip = given
            pairs = [(ids, into[0])]
            half = into[1].shape[0]
            for n in range(6):
                words, column = pl.ds(n // 3 * half, half), pl.ds(first * LANES, LANES)
                pairs.append((table.at[n % 3, words, column], into[1].at[:, pl.ds(n * LANES, LANES)]))
            pairs.append((taps.at[:, :, own], into[2]))
            for ref, target in zip((residue, decay, skip), into[3:]):
                pairs.append((ref.at[:, own], target))
            return [pltpu.make_async_copy(x, y, sem.at[which, n]) for n, (x, y) in enumerate(pairs)]

        now = bring(piece, held, 0)
        later = bring(piece + 1, ahead, 1) if ahead else []
        for copy in now:
            copy.start()
        for copy in now:
            copy.wait()
        for copy in later:
            copy.start()
    else:
        held, later = given, []
    compute(place, sends, held, outs, *refs)
    for copy in later:
        copy.wait()


def compute(place, sends, held, outs, halo, query, gated, inputs, gains, result, *streams):
    ids, table, taps, residue, decay, skip = held
    length = ids.shape[0] * ids.shape[1]
    steps = length // RUNS
    half = table.shape[0]
    width = taps.shape[1]
    modes = residue.shape[0]
    rim = width - 1
    tile = (RUNS, LANES)
    spread = lambda row: jnp.broadcast_to(row, tile)

    cols = ids.shape[1]
    part = cols // len(streams)
    word = lax.broadcasted_iota(jnp.int32, (RUNS, half), 1)

    def look_up(here, first, count, place_row):
        upper = here >= half
        within = jnp.where(upper, here - half, here)
        hot = [
            jnp.where(jnp.broadcast_to(within[:, j : j + 1], word.shape) == word, 1.0, 0.0)
            for j in range(first, first + count)
        ]
        hot = jnp.concatenate(hot, axis=0).astype(jnp.bfloat16)
        found = jnp.dot(hot, table[...], preferred_element_type=jnp.float32)
        for j in range(count):
            above = spread(here[:, first + j : first + j + 1]) >= half
            rows = found[j * RUNS : (j + 1) * RUNS]
            for k in range(3):
                low, high = (rows[:, n * LANES : (n + 1) * LANES] for n in (k, k + 3))
                place_row(k, j, jnp.where(above, high, low))

    def ids_of(block):
        return ids[pl.ds(block, RUNS, stride=steps // cols), :]

    def place_tail(k, j, row):
        halo[k, j * RUNS : (j + 1) * RUNS, :] = delay_runs(row, 1)

    look_up(ids_of(steps // cols - 1), cols - rim, rim, place_tail)

    filters = [[spread(taps[k, lag : lag + 1, :]) for lag in range(width)] for k in range(3)]

    def block_step(block, _):
        here = ids_of(block)
        seen = {}

        def row(k, j):
            if (k, j) not in seen:
                if j < 0:
                    seen[k, j] = halo[k, (rim + j) * RUNS : (rim + j + 1) * RUNS, :]
                else:
                    first = j % part * RUNS
                    seen[k, j] = streams[j // part][k, first : first + RUNS, :]
            return seen[k, j]

        def mix(first):
            for j in range(first, first + part):
                mixed = [
                    tree_sum([filters[k][lag] * row(k, j - lag) for lag in range(width)]) for k in range(3)
                ]
                at = pl.ds(pl.multiple_of((block * cols + j) * RUNS, RUNS), RUNS)
                query[at, :] = mixed[0]
                gated[at, :] = mixed[1] * mixed[2]

        for n, stream in enumerate(streams):

            def place_row(k, j, row, stream=stream):
                stream[k, j * RUNS : (j + 1) * RUNS, :] = row

            look_up(here, n * part, part, place_row)
            if n > 0:
                mix((n - 1) * part)
        mix(cols - part)
        for k in range(3):
            halo[k] = streams[-1][k, (part - rim) * RUNS :, :]
        return 0

    lax.fori_loop(0, steps // cols, block_step, 0)

    batch = steps // inputs.shape[0]
    unroll = max(32 // batch, 1)
    rate = decay[...] / length
    weight = residue[...] * jnp.sqrt(2.0 * rate)
    pole = jnp.exp(-rate)
    power = weight
    early = []
    for n in range(batch):
        early.append(spread(jnp.sum(power, axis=0, keepdims=True)))
        power = weight * jnp.exp(-rate * (n + 1))
    early[0] = early[0] + spread(skip[...])
    poles = [spread(pole[s : s + 1]) for s in range(modes)]
    leap = jnp.exp(-rate * batch)
    leaps = [spread(leap[s : s + 1]) for s in range(modes)]

    def tokens(ref, m):
        first = m * batch
        return [ref[pl.ds(pl.multiple_of((first + n) * RUNS, RUNS), RUNS), :] for n in range(batch)]

    def advance(m, state):
        values = tokens(gated, m)
        after = []
        for s in range(modes):
            taken = values[0]
            for value in values[1:]:
                taken = poles[s] * taken + value
            inputs[m, s * RUNS : (s + 1) * RUNS, :] = taken
            after.append(leaps[s] * state[s] + taken)
        return tuple(after)

    zero = jnp.zeros(tile, jnp.float32)
    ends = lax.fori_loop(0, steps // batch, advance, (zero,) * modes, unroll=unroll)
    begins = []
    for s in range(modes):
        value = delay_runs(ends[s], 1)
        by = 1
        while by < RUNS:
            value = value + spread(jnp.exp(-rate[s : s + 1] * (steps * by))) * delay_runs(value, by)
            by *= 2
        begins.append(value)

    weights = [spread(weight[s : s + 1]) for s in range(modes)]
    for s in range(modes):
        gains[s] = weights[s]

    def emit(m, terms):
        values = tokens(gated, m)
        answers = []
        for n, asked in enumerate(tokens(query, m)):
            terms = [p * x for p, x in zip(poles, terms)]
            close = [early[lag] * values[n - lag] for lag in range(n + 1)]
            answers.append(asked * tree_sum(close + terms))
        for n, answer in enumerate(answers):
            result[pl.ds(m * batch + n, RUNS, stride=steps), :] = answer
        return tuple(x + gains[s] * inputs[m, s * RUNS : (s + 1) * RUNS, :] for s, x in enumerate(terms))

    lax.fori_loop(0, steps // batch, emit, tuple(w * x for w, x in zip(weights, begins)), unroll=unroll)
    for out, hops in zip(outs, sends):
        size = out.shape[0] // len(hops)
        for n, hop in enumerate(hops):
            first = 0 if hop is None else pl.multiple_of(jnp.bitwise_xor(place, hop) * size, size)
            out[n * size : (n + 1) * size, :] = result[pl.ds(first, size), :].astype(jnp.bfloat16)


def run_operator(given, piece, pieces, sends, places, sliced):
    ids, table, taps, residue = given[:4]
    raw = piece == 0 or pieces > 2
    ahead = piece == 0 and pieces == 2
    vocab, modes, width = table.shape[-2], residue.shape[0], taps.shape[1]
    length = ids.size
    steps = length // RUNS
    cols = ids.shape[1]
    parts = max(cols // 32, 1)
    batch = max(4, steps // 128)
    inside = pl.BlockSpec(memory_space=pltpu.VMEM)
    outside = pl.BlockSpec(memory_space=pltpu.HBM)
    floats = lambda *shape: pltpu.VMEM(shape + (LANES,), jnp.float32)
    own = [
        jax.ShapeDtypeStruct(ids.shape, jnp.int32),
        jax.ShapeDtypeStruct((vocab // 2, 6 * LANES), jnp.bfloat16),
        jax.ShapeDtypeStruct((3, width, LANES), jnp.float32),
        jax.ShapeDtypeStruct((modes, LANES), jnp.float32),
        jax.ShapeDtypeStruct((modes, LANES), jnp.float32),
        jax.ShapeDtypeStruct((1, LANES), jnp.float32),
    ]
    rows = [length if hops == [None] else length // places * len(hops) for hops in sends]
    out_shape = [jax.ShapeDtypeStruct((count, LANES), jnp.bfloat16) for count in rows]
    scratch = []
    if raw:
        scratch = [pltpu.VMEM(x.shape, x.dtype) for x in own] + [pltpu.SemaphoreType.DMA((2, 11))]
        out_shape = out_shape + (own if ahead else [])
    scratch += [
        floats(3, (width - 1) * RUNS),
        floats(length),
        floats(length),
        floats(steps // batch, modes * RUNS),
        floats(modes, RUNS),
        floats(length),
    ]
    scratch += [floats(3, cols // parts * RUNS)] * parts
    held = scratch + own * 2 + out_shape
    room = sum(math.prod(x.shape) * jnp.dtype(x.dtype).itemsize for x in held if x.dtype in (jnp.float32, jnp.bfloat16))
    results = pl.pallas_call(
        functools.partial(operator, (piece, pieces, sends, sliced, raw, ahead)),
        in_specs=[outside if raw else inside] * 6,
        out_specs=[inside] * len(out_shape),
        out_shape=out_shape,
        scratch_shapes=scratch,
        compiler_params=pltpu.CompilerParams(vmem_limit_bytes=room + 4 * 2**20),
        cost_estimate=pl.CostEstimate(flops=length * LANES * 8000, bytes_accessed=4 * 2**20, transcendentals=0),
    )(*(given if not raw else [pltpu.with_memory_space_constraint(x, pltpu.HBM) for x in given]))
    return results[: len(sends)], results[len(sends) :]


def run_join(places, blocks, out):
    arrays = [array for array, _ in blocks]
    into = [] if out is None else [out]
    local, kept = arrays[0].shape[-2:]
    count = sum(len(marks) - marks.count(None) for _, marks in blocks)

    def kernel(*refs):
        refs = list(refs)
        if into:
            refs.pop(len(arrays))
        *refs, out, sem = refs
        place = lax.axis_index("seq")
        copies = []
        for ref, (_, marks) in zip(refs, blocks):
            for n, mark in enumerate(marks):
                if mark is None:
                    continue
                piece, hop, *plain = mark
                first = ((hop if plain else jnp.bitwise_xor(place, hop)) * 2 + piece) * kept
                target = out.at[:, pl.ds(first if plain else pl.multiple_of(first, kept), kept)]
                copies.append(pltpu.make_async_copy(ref.at[n], target, sem.at[len(copies)]))
        for copy in copies:
            copy.start()
        for copy in copies:
            copy.wait()

    anywhere = pl.BlockSpec(memory_space=pl.ANY)
    return pl.pallas_call(
        kernel,
        in_specs=[anywhere] * (len(arrays) + len(into)),
        out_specs=anywhere,
        out_shape=jax.ShapeDtypeStruct((local, places * 2 * kept), arrays[0].dtype),
        scratch_shapes=[pltpu.SemaphoreType.DMA((count,))],
        input_output_aliases={len(arrays): 0} if into else {},
        cost_estimate=pl.CostEstimate(flops=0, bytes_accessed=2**23, transcendentals=0),
        compiler_params=pltpu.CompilerParams(vmem_limit_bytes=2**20),
    )(*(pltpu.with_memory_space_constraint(x, pltpu.VMEM) for x in arrays), *into)


def by_hops(given, places, local):
    far = list(range(0, places, 4))
    hop = lambda x, by: lax.ppermute(x, "seq", [(i, i ^ by) for i in range(places)])

    def run(given, piece, sends):
        results, ahead = run_operator(given, piece, 2, sends, places, False)
        return [x.reshape(-1, local, x.shape[-1]) for x in results], ahead

    first, given = run(given, 0, [[d + e for e in range(4)] for d in far])
    landed = [hop(x, d) for x, d in zip(first[:0:-1], far[:0:-1])]
    landed = first[:1] + landed[::-1]
    sends = [[d, d + 1] for d in far] + [[d + e for d in far[1:] for e in (2, 3)], [2, 3]]
    (*straight, across, beside), _ = run(given, 1, sends)
    landed, straight = lax.optimization_barrier((landed, straight))
    crossed = hop(across, 2)
    final = [
        hop(jnp.concatenate([straight[n], crossed[2 * n - 2 : 2 * n]]), far[n]) for n in range(len(far) - 1, 0, -1)
    ][::-1]
    turn = jnp.concatenate([x[2:] for x in landed] + [beside])
    turn, crossed = lax.optimization_barrier((turn, crossed))
    turned = hop(turn, 2)
    paired = hop(jnp.concatenate([straight[0][1:2]] + [x[n : n + 1] for x in final for n in (1, 3)]), 1)
    out = run_join(
        places,
        [(x, [(0, d)]) for x, d in zip(landed, far)]
        + [(straight[0], [(1, 0)])]
        + [(x, [(1, d), None, (1, d + 2)]) for x, d in zip(final, far[1:])],
        None,
    )
    odd = [x[1:2] for x in landed] + [turned[n : n + 1] for n in range(1, turn.shape[0], 2)]
    return run_join(
        places,
        [(turned, [mark for d in far for mark in ((0, d + 2), None)] + [(1, 2)])]
        + [(paired, [(1, 1)] + [(1, d + e) for d in far[1:] for e in (1, 3)])]
        + [(hop(jnp.concatenate(odd), 1), [(0, d + 1) for d in far] + [(0, d + 3) for d in far] + [(1, 3)])],
        out,
    )


def body(token_ids, vocab_table, short_filter, residue, decay, skip_gain):
    places = lax.axis_size("seq")
    place = lax.axis_index("seq")
    length = token_ids.shape[0]
    local = length // places
    share = vocab_table.shape[2]
    pieces = -(-share // LANES)
    ids = token_ids.reshape(-1, min(LANES, length // RUNS))
    table = vocab_table.transpose(1, 0, 2)
    rows = [short_filter.transpose(1, 0, 2), residue.T, decay.T, skip_gain[None]]
    sliced = share % LANES != 0
    if sliced:
        widen = lambda x: jnp.pad(x, [(0, 0)] * (x.ndim - 1) + [(0, pieces * LANES - share)])
        rows = [widen(lax.dynamic_slice_in_dim(x, place * share, share, x.ndim - 1)) for x in rows]
        table = widen(table)
    given = (ids, table, *rows)
    if not sliced and pieces == 2 and places % 4 == 0 and places & (places - 1) == 0 and places > 4:
        return by_hops(given, places, local)
    parts = []
    for piece in range(pieces):
        blocks, ahead = run_operator(given, piece, pieces, [[None]], places, sliced)
        given = ahead or given
        kept = min(LANES, share - piece * LANES)
        sent = blocks[0][:, :kept].reshape(places, local, kept)
        parts.append(lax.all_to_all(sent, "seq", split_axis=0, concat_axis=0, tiled=True))
    return jnp.concatenate(parts, axis=2).transpose(1, 0, 2).reshape(local, places * share)


def solution(mesh):
    placed = (P("groups"), P(None, None, "seq"), P(), P(), P(), P())
    return jax.shard_map(
        body, mesh=mesh, in_specs=placed, out_specs=P(("groups", "seq"), None), check_vma=False
    )
```

```python
import functools
import math

import jax
import jax.numpy as jnp
from jax import lax
from jax.experimental import pallas as pl
from jax.experimental.pallas import tpu as pltpu
from jax.sharding import PartitionSpec as P

LANES = 128
RUNS = 8


def tree_sum(terms):
    while len(terms) > 1:
        pairs = [a + b for a, b in zip(terms[::2], terms[1::2])]
        terms = pairs + ([terms[-1]] if len(terms) % 2 else [])
    return terms[0]


def delay_runs(value, by):
    moved = pltpu.roll(value, by, 0)
    return jnp.where(lax.broadcasted_iota(jnp.int32, value.shape, 0) < by, 0.0, moved)


def operator(spot, *refs):
    piece, pieces, sends, sliced, raw, ahead = spot
    place = lax.axis_index("seq")
    refs = list(refs)
    take = lambda count: [refs.pop(0) for _ in range(count)]
    given, outs = take(6), take(len(sends))
    ahead = take(6) if ahead else []
    if raw:
        held, sem = take(6), take(1)[0]

        def bring(first, into, which):
            column = first * LANES if sliced else (place * pieces + first) * LANES
            own = pl.ds(pl.multiple_of(column, LANES), LANES)
            ids, table, taps, residue, decay, skip = given
            pairs = [(ids, into[0])]
            half = into[1].shape[0]
            for n in range(6):
                words, column = pl.ds(n // 3 * half, half), pl.ds(first * LANES, LANES)
                pairs.append((table.at[n % 3, words, column], into[1].at[:, pl.ds(n * LANES, LANES)]))
            pairs.append((taps.at[:, :, own], into[2]))
            for ref, target in zip((residue, decay, skip), into[3:]):
                pairs.append((ref.at[:, own], target))
            return [pltpu.make_async_copy(x, y, sem.at[which, n]) for n, (x, y) in enumerate(pairs)]

        now = bring(piece, held, 0)
        later = bring(piece + 1, ahead, 1) if ahead else []
        for copy in now:
            copy.start()
        now[0].wait()
    else:
        held, now, later = given, [], []
    compute(place, sends, held, outs, now[1:7], now[7:], later, *refs)
    for copy in later:
        copy.wait()


def compute(place, sends, held, outs, words, rows, later, halo, query, gated, inputs, gains, result, *streams):
    ids, table, taps, residue, decay, skip = held
    length = ids.shape[0] * ids.shape[1]
    steps = length // RUNS
    half = table.shape[0]
    width = taps.shape[1]
    modes = residue.shape[0]
    rim = width - 1
    tile = (RUNS, LANES)
    spread = lambda row: jnp.broadcast_to(row, tile)

    cols = ids.shape[1]
    part = cols // len(streams)
    word = lax.broadcasted_iota(jnp.int32, (RUNS, half), 1)

    def look_up(here, first, count, place_row, copies=()):
        upper = here >= half
        within = jnp.where(upper, here - half, here)
        hot = [
            jnp.where(jnp.broadcast_to(within[:, j : j + 1], word.shape) == word, 1.0, 0.0)
            for j in range(first, first + count)
        ]
        hot = jnp.concatenate(hot, axis=0).astype(jnp.bfloat16)
        for copy in copies:
            copy.wait()
        found = jnp.dot(hot, table[...], preferred_element_type=jnp.float32)
        for j in range(count):
            above = spread(here[:, first + j : first + j + 1]) >= half
            line = found[j * RUNS : (j + 1) * RUNS]
            for k in range(3):
                low, high = (line[:, n * LANES : (n + 1) * LANES] for n in (k, k + 3))
                place_row(k, j, jnp.where(above, high, low))

    def ids_of(block):
        return ids[pl.ds(block, RUNS, stride=steps // cols), :]

    def place_tail(k, j, row):
        halo[k, j * RUNS : (j + 1) * RUNS, :] = delay_runs(row, 1)

    look_up(ids_of(steps // cols - 1), cols - rim, rim, place_tail, words)
    for copy in rows:
        copy.wait()
    for copy in later:
        copy.start()

    filters = [[spread(taps[k, lag : lag + 1, :]) for lag in range(width)] for k in range(3)]

    def block_step(block, _):
        here = ids_of(block)
        seen = {}

        def row(k, j):
            if (k, j) not in seen:
                if j < 0:
                    seen[k, j] = halo[k, (rim + j) * RUNS : (rim + j + 1) * RUNS, :]
                else:
                    first = j % part * RUNS
                    seen[k, j] = streams[j // part][k, first : first + RUNS, :]
            return seen[k, j]

        def mix(first):
            for j in range(first, first + part):
                mixed = [
                    tree_sum([filters[k][lag] * row(k, j - lag) for lag in range(width)]) for k in range(3)
                ]
                at = pl.ds(pl.multiple_of((block * cols + j) * RUNS, RUNS), RUNS)
                query[at, :] = mixed[0]
                gated[at, :] = mixed[1] * mixed[2]

        for n, stream in enumerate(streams):

            def place_row(k, j, row, stream=stream):
                stream[k, j * RUNS : (j + 1) * RUNS, :] = row

            look_up(here, n * part, part, place_row)
            if n > 0:
                mix((n - 1) * part)
        mix(cols - part)
        for k in range(3):
            halo[k] = streams[-1][k, (part - rim) * RUNS :, :]
        return 0

    lax.fori_loop(0, steps // cols, block_step, 0)

    batch = steps // inputs.shape[0]
    unroll = max(32 // batch, 1)
    rate = decay[...] / length
    weight = residue[...] * jnp.sqrt(2.0 * rate)
    pole = jnp.exp(-rate)
    power = weight
    early = []
    for n in range(batch):
        early.append(spread(jnp.sum(power, axis=0, keepdims=True)))
        power = weight * jnp.exp(-rate * (n + 1))
    early[0] = early[0] + spread(skip[...])
    poles = [spread(pole[s : s + 1]) for s in range(modes)]
    leap = jnp.exp(-rate * batch)
    leaps = [spread(leap[s : s + 1]) for s in range(modes)]

    def tokens(ref, m):
        first = m * batch
        return [ref[pl.ds(pl.multiple_of((first + n) * RUNS, RUNS), RUNS), :] for n in range(batch)]

    def advance(m, state):
        values = tokens(gated, m)
        after = []
        for s in range(modes):
            taken = values[0]
            for value in values[1:]:
                taken = poles[s] * taken + value
            inputs[m, s * RUNS : (s + 1) * RUNS, :] = taken
            after.append(leaps[s] * state[s] + taken)
        return tuple(after)

    zero = jnp.zeros(tile, jnp.float32)
    ends = lax.fori_loop(0, steps // batch, advance, (zero,) * modes, unroll=unroll)
    begins = []
    for s in range(modes):
        value = delay_runs(ends[s], 1)
        by = 1
        while by < RUNS:
            value = value + spread(jnp.exp(-rate[s : s + 1] * (steps * by))) * delay_runs(value, by)
            by *= 2
        begins.append(value)

    weights = [spread(weight[s : s + 1]) for s in range(modes)]
    for s in range(modes):
        gains[s] = weights[s]

    def emit(m, terms):
        values = tokens(gated, m)
        answers = []
        for n, asked in enumerate(tokens(query, m)):
            terms = [p * x for p, x in zip(poles, terms)]
            close = [early[lag] * values[n - lag] for lag in range(n + 1)]
            answers.append(asked * tree_sum(close + terms))
        for n, answer in enumerate(answers):
            result[pl.ds(m * batch + n, RUNS, stride=steps), :] = answer
        return tuple(x + gains[s] * inputs[m, s * RUNS : (s + 1) * RUNS, :] for s, x in enumerate(terms))

    lax.fori_loop(0, steps // batch, emit, tuple(w * x for w, x in zip(weights, begins)), unroll=unroll)
    for out, hops in zip(outs, sends):
        size = out.shape[0] // len(hops)
        for n, hop in enumerate(hops):
            first = 0 if hop is None else pl.multiple_of(jnp.bitwise_xor(place, hop) * size, size)
            out[n * size : (n + 1) * size, :] = result[pl.ds(first, size), :].astype(jnp.bfloat16)


def run_operator(given, piece, pieces, sends, places, sliced):
    ids, table, taps, residue = given[:4]
    raw = piece == 0 or pieces > 2
    ahead = piece == 0 and pieces == 2
    vocab, modes, width = table.shape[-2], residue.shape[0], taps.shape[1]
    length = ids.size
    steps = length // RUNS
    cols = ids.shape[1]
    parts = max(cols // 32, 1)
    batch = max(4, steps // 128)
    inside = pl.BlockSpec(memory_space=pltpu.VMEM)
    outside = pl.BlockSpec(memory_space=pltpu.HBM)
    floats = lambda *shape: pltpu.VMEM(shape + (LANES,), jnp.float32)
    own = [
        jax.ShapeDtypeStruct(ids.shape, jnp.int32),
        jax.ShapeDtypeStruct((vocab // 2, 6 * LANES), jnp.bfloat16),
        jax.ShapeDtypeStruct((3, width, LANES), jnp.float32),
        jax.ShapeDtypeStruct((modes, LANES), jnp.float32),
        jax.ShapeDtypeStruct((modes, LANES), jnp.float32),
        jax.ShapeDtypeStruct((1, LANES), jnp.float32),
    ]
    rows = [length if hops == [None] else length // places * len(hops) for hops in sends]
    out_shape = [jax.ShapeDtypeStruct((count, LANES), jnp.bfloat16) for count in rows]
    scratch = []
    if raw:
        scratch = [pltpu.VMEM(x.shape, x.dtype) for x in own] + [pltpu.SemaphoreType.DMA((2, 11))]
        out_shape = out_shape + (own if ahead else [])
    scratch += [
        floats(3, (width - 1) * RUNS),
        floats(length),
        floats(length),
        floats(steps // batch, modes * RUNS),
        floats(modes, RUNS),
        floats(length),
    ]
    scratch += [floats(3, cols // parts * RUNS)] * parts
    held = scratch + own * 2 + out_shape
    room = sum(math.prod(x.shape) * jnp.dtype(x.dtype).itemsize for x in held if x.dtype in (jnp.float32, jnp.bfloat16))
    results = pl.pallas_call(
        functools.partial(operator, (piece, pieces, sends, sliced, raw, ahead)),
        in_specs=[outside if raw else inside] * 6,
        out_specs=[inside] * len(out_shape),
        out_shape=out_shape,
        scratch_shapes=scratch,
        compiler_params=pltpu.CompilerParams(vmem_limit_bytes=room + 4 * 2**20),
        cost_estimate=pl.CostEstimate(flops=length * LANES * 8000, bytes_accessed=4 * 2**20, transcendentals=0),
    )(*(given if not raw else [pltpu.with_memory_space_constraint(x, pltpu.HBM) for x in given]))
    return results[: len(sends)], results[len(sends) :]


def run_join(places, blocks, out):
    arrays = [array for array, _ in blocks]
    into = [] if out is None else [out]
    local, kept = arrays[0].shape[-2:]
    count = sum(len(marks) - marks.count(None) for _, marks in blocks)

    def kernel(*refs):
        refs = list(refs)
        if into:
            refs.pop(len(arrays))
        *refs, out, sem = refs
        place = lax.axis_index("seq")
        copies = []
        for ref, (_, marks) in zip(refs, blocks):
            for n, mark in enumerate(marks):
                if mark is None:
                    continue
                piece, hop, *plain = mark
                first = ((hop if plain else jnp.bitwise_xor(place, hop)) * 2 + piece) * kept
                target = out.at[:, pl.ds(first if plain else pl.multiple_of(first, kept), kept)]
                copies.append(pltpu.make_async_copy(ref.at[n], target, sem.at[len(copies)]))
        for copy in copies:
            copy.start()
        for copy in copies:
            copy.wait()

    anywhere = pl.BlockSpec(memory_space=pl.ANY)
    return pl.pallas_call(
        kernel,
        in_specs=[anywhere] * (len(arrays) + len(into)),
        out_specs=anywhere,
        out_shape=jax.ShapeDtypeStruct((local, places * 2 * kept), arrays[0].dtype),
        scratch_shapes=[pltpu.SemaphoreType.DMA((count,))],
        input_output_aliases={len(arrays): 0} if into else {},
        cost_estimate=pl.CostEstimate(flops=0, bytes_accessed=2**23, transcendentals=0),
        compiler_params=pltpu.CompilerParams(vmem_limit_bytes=2**20),
    )(*(pltpu.with_memory_space_constraint(x, pltpu.VMEM) for x in arrays), *into)


def by_hops(given, places, local):
    far = list(range(0, places, 4))
    hop = lambda x, by: lax.ppermute(x, "seq", [(i, i ^ by) for i in range(places)])

    def run(given, piece, sends):
        results, ahead = run_operator(given, piece, 2, sends, places, False)
        return [x.reshape(-1, local, x.shape[-1]) for x in results], ahead

    first, given = run(given, 0, [[d + e for e in range(4)] for d in far])
    landed = [hop(x, d) for x, d in zip(first[:0:-1], far[:0:-1])]
    landed = first[:1] + landed[::-1]
    sends = [[d, d + 1] for d in far] + [[d + e for d in far[1:] for e in (2, 3)], [2, 3]]
    (*straight, across, beside), _ = run(given, 1, sends)
    landed, straight = lax.optimization_barrier((landed, straight))
    crossed = hop(across, 2)
    final = [
        hop(jnp.concatenate([straight[n], crossed[2 * n - 2 : 2 * n]]), far[n]) for n in range(len(far) - 1, 0, -1)
    ][::-1]
    turn = jnp.concatenate([x[2:] for x in landed] + [beside])
    turn, crossed = lax.optimization_barrier((turn, crossed))
    turned = hop(turn, 2)
    paired = hop(jnp.concatenate([straight[0][1:2]] + [x[n : n + 1] for x in final for n in (1, 3)]), 1)
    out = run_join(
        places,
        [(x, [(0, d)]) for x, d in zip(landed, far)]
        + [(straight[0], [(1, 0)])]
        + [(x, [(1, d), None, (1, d + 2)]) for x, d in zip(final, far[1:])],
        None,
    )
    odd = [x[1:2] for x in landed] + [turned[n : n + 1] for n in range(1, turn.shape[0], 2)]
    return run_join(
        places,
        [(turned, [mark for d in far for mark in ((0, d + 2), None)] + [(1, 2)])]
        + [(paired, [(1, 1)] + [(1, d + e) for d in far[1:] for e in (1, 3)])]
        + [(hop(jnp.concatenate(odd), 1), [(0, d + 1) for d in far] + [(0, d + 3) for d in far] + [(1, 3)])],
        out,
    )


def body(token_ids, vocab_table, short_filter, residue, decay, skip_gain):
    places = lax.axis_size("seq")
    place = lax.axis_index("seq")
    length = token_ids.shape[0]
    local = length // places
    share = vocab_table.shape[2]
    pieces = -(-share // LANES)
    ids = token_ids.reshape(-1, min(LANES, length // RUNS))
    table = vocab_table.transpose(1, 0, 2)
    rows = [short_filter.transpose(1, 0, 2), residue.T, decay.T, skip_gain[None]]
    sliced = share % LANES != 0
    if sliced:
        widen = lambda x: jnp.pad(x, [(0, 0)] * (x.ndim - 1) + [(0, pieces * LANES - share)])
        rows = [widen(lax.dynamic_slice_in_dim(x, place * share, share, x.ndim - 1)) for x in rows]
        table = widen(table)
    given = (ids, table, *rows)
    if not sliced and pieces == 2 and places % 4 == 0 and places & (places - 1) == 0 and places > 4:
        return by_hops(given, places, local)
    parts = []
    for piece in range(pieces):
        blocks, ahead = run_operator(given, piece, pieces, [[None]], places, sliced)
        given = ahead or given
        kept = min(LANES, share - piece * LANES)
        sent = blocks[0][:, :kept].reshape(places, local, kept)
        parts.append(lax.all_to_all(sent, "seq", split_axis=0, concat_axis=0, tiled=True))
    return jnp.concatenate(parts, axis=2).transpose(1, 0, 2).reshape(local, places * share)


def solution(mesh):
    placed = (P("groups"), P(None, None, "seq"), P(), P(), P(), P())
    return jax.shard_map(
        body, mesh=mesh, in_specs=placed, out_specs=P(("groups", "seq"), None), check_vma=False
    )
```
